768 devices in a mesh: row: 4 (over x), col: 96 (over z, y), layer: 2 (over core).
Axes of the slice: x: 4, y: 8, z: 12, core: 2. Of those that a mesh axis runs over, the one named last changes fastest.
Arguments:
- values: bfloat16 [1536, 10, 128, 128], P(('row', 'col'), None, 'layer'), may hold values from -0.8984375 to 0.8984375
- columns: int32 [1536, 10], replicated, may hold values from 0 to 1535, as said below
Outputs:
- square: bfloat16 [1536, 10, 128, 128], P(('row', 'col'), None, 'layer')
The draws below stay inside these ranges and needn't reach their ends.
Inputs may be any that keep to these rules, and one draw needn't show every extreme that they name: `columns`: each row's 10 entries are distinct, and each lies within 12 of the row's index, counted cyclically modulo 1536.
All inputs are finite; a program needn't handle non-finite values.
Results may differ from the reference program's by a relative error of at most 0.001.
Values may be sent and summed in bfloat16 or wider, within the bound.
A program may use at most 64 MiB of HBM per device.

```python
import jax
import jax.numpy as jnp
from jax import lax

B = 128
K = 10
ROWS_DEV = 4
NB = 1536


def draw_columns(key, part):
    key = jax.random.fold_in(key, 11)
    row_keys = jax.random.split(key, NB)
    reach = 3 * ROWS_DEV
    offsets = jax.vmap(lambda one_key: jax.random.permutation(one_key, 2 * reach + 1)[:K])(row_keys) - reach
    return ((jnp.arange(NB, dtype=jnp.int32)[:, None] + offsets) % NB).astype(jnp.int32)


def steps_of(stream_key, dims, pieces, low, top_value):
    factor_of, own = 1.0, jax.random.fold_in(stream_key, 6)
    for position, parts in pieces:
        heights = jnp.exp(jax.random.uniform(jax.random.fold_in(own, position), (parts,), jnp.float32, low / len(pieces), top_value / len(pieces)))
        factor_of = factor_of * jnp.repeat(heights, dims[position] // parts).reshape([-1 if axis == position else 1 for axis in range(len(dims))])
    return factor_of


def gaussian(stream_key, dims, scale, bound, cuts=(), held_as=jnp.bfloat16):
    entries = jax.random.normal(stream_key, dims, jnp.float32) * scale
    if len(cuts) > 0:
        entries = steps_of(stream_key, dims, cuts, -0.22, 0.18) * entries
    return jnp.clip(entries, min=-bound, max=bound).astype(held_as)


def setup_inputs(seed: int = 0) -> dict:
    streams_of = jax.random.split(jax.random.key(seed), 3)
    return {
        "values": gaussian(streams_of[0], (NB, K, B, B), 0.15, 0.8984375, ((0, 384), (2, 2))),
        "columns": draw_columns(jax.random.fold_in(streams_of[2], 71), 0),
    }


def reference(values, columns):
    slot_range = jnp.arange(K, dtype=jnp.int32)

    def one_row(item):
        row_values, row_columns = item
        block_columns = columns[row_columns]
        matches = block_columns[:, :, None] == row_columns[None, None, :]
        slot_index = jnp.sum(jnp.where(matches, slot_range[None, :, None], 0), axis=1).astype(jnp.int32)
        present = jnp.any(matches, axis=1)
        near_values = values[row_columns]
        chosen = jnp.take_along_axis(near_values, slot_index[:, :, None, None], axis=1)
        chosen = jnp.where(present[:, :, None, None], chosen.astype(jnp.float32), jnp.float32(0.0))
        result = jnp.einsum("kab,kmbc->mac", row_values.astype(jnp.float32), chosen)
        return result.astype(jnp.bfloat16)

    return lax.map(one_row, (values, columns))
```

```python
import functools

import jax
import jax.numpy as jnp
from jax import lax
from jax.experimental import pallas as pl
from jax.experimental.pallas import tpu as pltpu
from jax.sharding import PartitionSpec as P

HOPS = 3


def square_kernel(sizes, columns_ref, values_ref, out_ref, near, own, table, place,
                  hop_send, hop_recv, core_send, core_recv, local_sem):
    rows_axis, cols_axis = sizes
    positions = rows_axis * cols_axis
    rows_here, slots, half, width = values_ref.shape
    total_rows = rows_here * positions
    row, col, layer = lax.axis_index("row"), lax.axis_index("col"), lax.axis_index("layer")
    position = row * cols_axis + col
    units = 2 * HOPS + 1
    empty = units * rows_here * slots

    def at(offset):
        there = lax.rem(position + offset + positions, positions)
        return (there // cols_axis, lax.rem(there, cols_axis), layer)

    sibling = (row, col, 1 - layer)
    my_half = pl.ds(pl.multiple_of(layer * half, half), half)

    def unit_rows(unit, r):
        return near.at[pl.ds((unit * rows_here + r) * slots, slots), my_half, :]

    def hop(h, direction, r):
        index = 0 if direction > 0 else 1
        source = values_ref.at[r] if h == 0 else unit_rows(HOPS - direction * h, r)
        return pltpu.make_async_remote_copy(
            source, unit_rows(HOPS - direction * (h + 1), r),
            hop_send.at[h, index, r], hop_recv.at[h, index, r],
            device_id=at(direction), device_id_type=pl.DeviceIdType.MESH)

    def across(unit, r):
        source = values_ref.at[r] if unit == HOPS else unit_rows(unit, r)
        return pltpu.make_async_remote_copy(
            source, unit_rows(unit, r), core_send.at[unit, r], core_recv.at[unit, r],
            device_id=sibling, device_id_type=pl.DeviceIdType.MESH)

    table_copy = pltpu.make_async_copy(columns_ref, table, local_sem.at[0])
    own_copy = pltpu.make_async_copy(values_ref, own, local_sem.at[1])
    table_copy.start()
    own_copy.start()

    barrier = pltpu.get_barrier_semaphore()
    for peer in (at(1), at(-1), sibling):
        pl.semaphore_signal(barrier, inc=1, device_id=peer, device_id_type=pl.DeviceIdType.MESH)
    pl.semaphore_wait(barrier, 3)

    for r in range(rows_here):
        for direction in (1, -1):
            hop(0, direction, r).start()
    for r in range(rows_here):
        across(HOPS, r).start()
    near[empty] = jnp.zeros((2 * half, width), near.dtype)
    near_own = [pltpu.make_async_copy(values_ref.at[r], unit_rows(HOPS, r), local_sem.at[2 + r]) for r in range(rows_here)]
    for copy in near_own:
        copy.start()
    table_copy.wait()

    @pl.loop(0, rows_here * slots)
    def _(step):
        t, k = step // slots, lax.rem(step, slots)
        i = position * rows_here + t
        j = table[k, i]
        base = lax.rem(j - position * rows_here + HOPS * rows_here + total_rows, total_rows) * slots
        there = [table[s, j] for s in range(slots)]
        for m in range(slots):
            wanted = table[m, i]
            found = empty
            for s in range(slots):
                found = jnp.where(there[s] == wanted, base + s, found)
            place[step * slots + m] = jnp.minimum(found, empty)

    for h in range(HOPS):
        for r in range(rows_here):
            for direction in (1, -1):
                hop(h, direction, r).wait_recv()
                if h + 1 < HOPS:
                    hop(h + 1, direction, r).start()
                across(HOPS - direction * (h + 1), r).start()
    own_copy.wait()
    for copy in near_own:
        copy.wait()
    for unit in range(units):
        for r in range(rows_here):
            across(unit, r).wait_recv()

    pairs = slots // 2

    @pl.loop(0, rows_here * pairs)
    def _(step):
        t, pair = step // pairs, lax.rem(step, pairs)
        left = jnp.concatenate([own[t, k] for k in range(slots)], axis=1)
        first = t * slots * slots + 2 * pair
        right = jnp.concatenate([
            jnp.concatenate([near[place[first + k * slots]], near[place[first + k * slots + 1]]], axis=1)
            for k in range(slots)], axis=0)
        product = jnp.dot(left, right, preferred_element_type=jnp.float32).astype(out_ref.dtype)
        out_ref[t, 2 * pair] = product[:, :width]
        out_ref[t, 2 * pair + 1] = product[:, width:]

    for h in range(HOPS):
        for r in range(rows_here):
            for direction in (1, -1):
                hop(h, direction, r).wait_send()
    for unit in range(units):
        for r in range(rows_here):
            across(unit, r).wait_send()


def on_device(sizes, values, columns):
    rows_here, slots, half, width = values.shape
    units = 2 * HOPS + 1
    return pl.pallas_call(
        functools.partial(square_kernel, sizes),
        out_shape=jax.ShapeDtypeStruct(values.shape, values.dtype),
        in_specs=[pl.BlockSpec(memory_space=pltpu.HBM), pl.BlockSpec(memory_space=pltpu.HBM)],
        out_specs=pl.BlockSpec(memory_space=pltpu.VMEM),
        scratch_shapes=[
            pltpu.VMEM((units * rows_here * slots + 1, 2 * half, width), values.dtype),
            pltpu.VMEM(values.shape, values.dtype),
            pltpu.SMEM(columns.shape[::-1], jnp.int32),
            pltpu.SMEM((rows_here * slots * slots,), jnp.int32),
            pltpu.SemaphoreType.DMA((HOPS, 2, rows_here)),
            pltpu.SemaphoreType.DMA((HOPS, 2, rows_here)),
            pltpu.SemaphoreType.DMA((units, rows_here)),
            pltpu.SemaphoreType.DMA((units, rows_here)),
            pltpu.SemaphoreType.DMA((2 + rows_here,)),
        ],
        compiler_params=pltpu.CompilerParams(
            collective_id=0, has_side_effects=True, vmem_limit_bytes=32 << 20),
        name="square",
    )(columns.T, values)


def solution(mesh):
    return jax.shard_map(
        functools.partial(on_device, (mesh.shape["row"], mesh.shape["col"])),
        mesh=mesh,
        in_specs=(P(("row", "col"), None, "layer", None), P()),
        out_specs=P(("row", "col"), None, "layer", None),
        check_vma=False,
    )
```

```python
import functools

import jax
import jax.numpy as jnp
from jax import lax
from jax.experimental import pallas as pl
from jax.experimental.pallas import tpu as pltpu
from jax.sharding import PartitionSpec as P

HOPS = 3
REACH = 12
SPAN = 2 * REACH
STREAM = 48
CHUNK = 8
LEAD = 2 * CHUNK
MESH = pl.DeviceIdType.MESH


def whole_kernel(sizes, columns_ref, values_ref, out_ref, near, own, table, place,
                 hop_send, hop_recv, core_send, core_recv, local_sem):
    rows_axis, cols_axis = sizes
    positions = rows_axis * cols_axis
    rows_here, slots, half, width = values_ref.shape
    total_rows = rows_here * positions
    row, col, layer = lax.axis_index("row"), lax.axis_index("col"), lax.axis_index("layer")
    position = row * cols_axis + col
    units = 2 * HOPS + 1
    empty = units * rows_here * slots

    def at(offset):
        there = lax.rem(position + offset + positions, positions)
        return (there // cols_axis, lax.rem(there, cols_axis), layer)

    sibling = (row, col, 1 - layer)
    my_half = pl.ds(pl.multiple_of(layer * half, half), half)

    def unit_rows(unit, r):
        return near.at[pl.ds((unit * rows_here + r) * slots, slots), my_half, :]

    def hop(h, direction, r):
        index = 0 if direction > 0 else 1
        source = values_ref.at[r] if h == 0 else unit_rows(HOPS - direction * h, r)
        return pltpu.make_async_remote_copy(
            source, unit_rows(HOPS - direction * (h + 1), r),
            hop_send.at[h, index, r], hop_recv.at[h, index, r],
            device_id=at(direction), device_id_type=MESH)

    def across(unit, r):
        source = values_ref.at[r] if unit == HOPS else unit_rows(unit, r)
        return pltpu.make_async_remote_copy(
            source, unit_rows(unit, r), core_send.at[unit, r], core_recv.at[unit, r],
            device_id=sibling, device_id_type=MESH)

    table_copy = pltpu.make_async_copy(columns_ref, table, local_sem.at[0])
    own_copy = pltpu.make_async_copy(values_ref, own, local_sem.at[1])
    table_copy.start()
    own_copy.start()

    barrier = pltpu.get_barrier_semaphore()
    for peer in (at(1), at(-1), sibling):
        pl.semaphore_signal(barrier, inc=1, device_id=peer, device_id_type=MESH)
    pl.semaphore_wait(barrier, 3)

    for r in range(rows_here):
        for direction in (1, -1):
            hop(0, direction, r).start()
    for r in range(rows_here):
        across(HOPS, r).start()
    near[empty] = jnp.zeros((2 * half, width), near.dtype)
    near_own = [pltpu.make_async_copy(values_ref.at[r], unit_rows(HOPS, r), local_sem.at[2 + r]) for r in range(rows_here)]
    for copy in near_own:
        copy.start()
    table_copy.wait()

    @pl.loop(0, rows_here * slots)
    def _(step):
        t, k = step // slots, lax.rem(step, slots)
        i = position * rows_here + t
        j = table[k, i]
        base = lax.rem(j - position * rows_here + HOPS * rows_here + total_rows, total_rows) * slots
        there = [table[s, j] for s in range(slots)]
        for m in range(slots):
            wanted = table[m, i]
            found = empty
            for s in range(slots):
                found = jnp.where(there[s] == wanted, base + s, found)
            place[step * slots + m] = jnp.minimum(found, empty)

    for h in range(HOPS):
        for r in range(rows_here):
            for direction in (1, -1):
                hop(h, direction, r).wait_recv()
                if h + 1 < HOPS:
                    hop(h + 1, direction, r).start()
                across(HOPS - direction * (h + 1), r).start()
    own_copy.wait()
    for copy in near_own:
        copy.wait()
    for unit in range(units):
        for r in range(rows_here):
            across(unit, r).wait_recv()

    pairs = slots // 2

    @pl.loop(0, rows_here * pairs)
    def _(step):
        t, pair = step // pairs, lax.rem(step, pairs)
        left = jnp.concatenate([own[t, k] for k in range(slots)], axis=1)
        first = t * slots * slots + 2 * pair
        right = jnp.concatenate([
            jnp.concatenate([near[place[first + k * slots]], near[place[first + k * slots + 1]]], axis=1)
            for k in range(slots)], axis=0)
        product = jnp.dot(left, right, preferred_element_type=jnp.float32).astype(out_ref.dtype)
        out_ref[t, 2 * pair] = product[:, :width]
        out_ref[t, 2 * pair + 1] = product[:, width:]

    for h in range(HOPS):
        for r in range(rows_here):
            for direction in (1, -1):
                hop(h, direction, r).wait_send()
    for unit in range(units):
        for r in range(rows_here):
            across(unit, r).wait_send()


def whole_square(sizes, table, values):
    rows_here, slots, half, width = values.shape
    units = 2 * HOPS + 1
    return pl.pallas_call(
        functools.partial(whole_kernel, sizes),
        out_shape=jax.ShapeDtypeStruct(values.shape, values.dtype),
        in_specs=[pl.BlockSpec(memory_space=pl.ANY), pl.BlockSpec(memory_space=pl.ANY)],
        out_specs=pl.BlockSpec(memory_space=pltpu.VMEM),
        scratch_shapes=[
            pltpu.VMEM((units * rows_here * slots + 1, 2 * half, width), values.dtype),
            pltpu.VMEM(values.shape, values.dtype),
            pltpu.SMEM(table.shape, jnp.int32),
            pltpu.SMEM((rows_here * slots * slots,), jnp.int32),
            pltpu.SemaphoreType.DMA((HOPS, 2, rows_here)),
            pltpu.SemaphoreType.DMA((HOPS, 2, rows_here)),
            pltpu.SemaphoreType.DMA((units, rows_here)),
            pltpu.SemaphoreType.DMA((units, rows_here)),
            pltpu.SemaphoreType.DMA((2 + rows_here,)),
        ],
        compiler_params=pltpu.CompilerParams(
            collective_id=1, has_side_effects=True, vmem_limit_bytes=56 << 20),
        name="whole_square",
    )(table, values)


def shifted_mask(mask, step):
    return mask << -step if step < 0 else mask >> step


def stream_lengths(table_ref, total_rows, rows_here):
    table = table_ref[...]
    lane = lax.broadcasted_iota(jnp.int32, table.shape, 1)
    place = table - lane + REACH
    place = jnp.where(place < 0, place + total_rows, place)
    place = jnp.where(place >= total_rows, place - total_rows, place)
    place = jnp.clip(place, 0, SPAN)
    masks = jnp.sum(jnp.left_shift(jnp.ones_like(place), place), axis=0, keepdims=True)
    masks = jnp.broadcast_to(masks, (8, total_rows))
    own_row = lax.broadcasted_iota(jnp.int32, masks.shape, 1) % rows_here

    def ahead(array, steps):
        return pltpu.roll(array, (-steps) % total_rows, 1)

    longest = jnp.zeros((1, total_rows), jnp.int32)
    for direction in (1, -1):
        wanted = {}
        for away in (2, 3):
            got = jnp.zeros_like(masks)
            for step in range(away * rows_here - rows_here + 1, away * rows_here + rows_here):
                if step > REACH:
                    continue
                step = direction * step
                there = ahead(masks, step)
                row_there = own_row + step - direction * away * rows_here
                use = (row_there >= 0) & (row_there < rows_here)
                use = use & (((there >> (REACH - step)) & 1) == 1)
                got = got | jnp.where(use, shifted_mask(there, -step), 0)
            wanted[away] = got[0:1]

        def count(mask):
            hits = jnp.sum((jnp.broadcast_to(mask, place.shape) >> place) & 1, axis=0, keepdims=True)
            hits = jnp.broadcast_to(hits, (8, total_rows))
            summed = hits
            for r in range(1, rows_here):
                summed = summed + ahead(hits, r)
            return summed

        first = jnp.maximum(count(wanted[2] | wanted[3]), LEAD)
        second = ahead(count(wanted[3]), -direction * rows_here)
        longest = jnp.maximum(longest, jnp.where(own_row == 0, first + second, 0)[0:1])
    return jnp.max(longest)


def sparse_kernel(sizes, columns_ref, values_ref, out_ref, longest_ref, mine, theirs, landed, packed, left_side,
                  table, table_rows, masks, needs, order, slot_of, place,
                  unit_send, unit_recv, stream_send, stream_recv, core_send, core_recv, local_sem):
    rows_axis, cols_axis = sizes
    positions = rows_axis * cols_axis
    blocks, half, width = values_ref.shape
    rows_here, slots = out_ref.shape[:2]
    total_rows = rows_here * positions
    row, col, layer = lax.axis_index("row"), lax.axis_index("col"), lax.axis_index("layer")
    position = row * cols_axis + col
    first_row = position * rows_here
    chunks = STREAM // CHUNK
    directions = (1, -1)
    unit_base = (blocks, 2 * blocks)
    stream_base = (3 * blocks, 3 * blocks + STREAM)
    empty = 3 * blocks + 2 * STREAM
    units = 2 * HOPS + 1

    def at(offset):
        there = lax.rem(position + offset + positions, positions)
        return (there // cols_axis, lax.rem(there, cols_axis), layer)

    sibling = (row, col, 1 - layer)

    def unit_copy(d, r):
        part = pl.ds(unit_base[d] + r * slots, slots)
        return pltpu.make_async_remote_copy(
            values_ref.at[pl.ds(r * slots, slots)], mine.at[part], unit_send.at[d, r], unit_recv.at[d, r],
            device_id=at(directions[d]), device_id_type=MESH)

    def stream_copy(d, c):
        part = pl.ds(c * CHUNK, CHUNK)
        return pltpu.make_async_remote_copy(
            packed.at[d, part], landed.at[d, part], stream_send.at[d, c], stream_recv.at[d, c],
            device_id=at(directions[d]), device_id_type=MESH)

    def own_across():
        return pltpu.make_async_remote_copy(
            values_ref, theirs.at[pl.ds(0, blocks)], core_send.at[0], core_recv.at[0],
            device_id=sibling, device_id_type=MESH)

    def unit_across(d, r):
        part = pl.ds(unit_base[d] + r * slots, slots)
        index = 1 + d * rows_here + r
        return pltpu.make_async_remote_copy(
            mine.at[part], theirs.at[part], core_send.at[index], core_recv.at[index],
            device_id=sibling, device_id_type=MESH)

    def stream_across(d, c):
        index = 1 + 2 * rows_here + d * chunks + c
        return pltpu.make_async_remote_copy(
            landed.at[d, pl.ds(c * CHUNK, CHUNK)], theirs.at[pl.ds(stream_base[d] + c * CHUNK, CHUNK)],
            core_send.at[index], core_recv.at[index], device_id=sibling, device_id_type=MESH)

    table_copy = pltpu.make_async_copy(columns_ref, table, local_sem.at[0])
    rows_copy = pltpu.make_async_copy(columns_ref, table_rows, local_sem.at[1])
    own_copy = pltpu.make_async_copy(values_ref, mine.at[pl.ds(0, blocks)], local_sem.at[2])
    table_copy.start()
    rows_copy.start()
    own_copy.start()

    barrier = pltpu.get_barrier_semaphore()
    for peer in (at(1), at(-1), sibling):
        pl.semaphore_signal(barrier, inc=1, device_id=peer, device_id_type=MESH)
    pl.semaphore_wait(barrier, 3)

    for r in range(rows_here):
        for d in range(2):
            unit_copy(d, r).start()
    own_across().start()
    mine[empty] = jnp.zeros((half, width), mine.dtype)
    theirs[empty] = jnp.zeros((half, width), mine.dtype)

    table_copy.wait()

    def wrapped(value):
        value = jnp.where(value < 0, value + total_rows, value)
        return jnp.where(value >= total_rows, value - total_rows, value)

    def distance(entry, i):
        return jnp.clip(wrapped(entry - i + REACH), 0, SPAN)

    @pl.loop(0, 5 * rows_here)
    def _(n):
        i = wrapped(first_row - 2 * rows_here + n)
        mask = jnp.int32(0)
        for k in range(slots):
            mask = mask | (jnp.int32(1) << distance(table[k, i], i))
        masks[n] = mask

    def need(source, receiver, r):
        got = jnp.int32(0)
        for t in range(rows_here):
            step = rows_here * (source - receiver) + r - t
            if abs(step) <= REACH:
                mask = masks[rows_here * (receiver + 2) + t]
                got = got | jnp.where(((mask >> (step + REACH)) & 1) == 1, shifted_mask(mask, step), 0)
        return got

    for d, sign in enumerate(directions):
        pairs = ((-1, 1), (-1, 2), (-2, 0), (-2, 1), (-3, 0))
        for n, (source, receiver) in enumerate(pairs):
            for r in range(rows_here):
                needs[(d * len(pairs) + n) * rows_here + r] = need(sign * source, sign * receiver, r)

        def flag(n, r, e):
            return (needs[(d * len(pairs) + n) * rows_here + r] >> e) & 1

        def of_block(source, step):
            r, s = step // slots, lax.rem(step, slots)
            j = wrapped(first_row + sign * source * rows_here + r)
            return r, distance(table[s, j], j)

        word = blocks // 2

        def gather(step, carry):
            far_low, far_high, near_low, near_high, count = carry
            r, e = of_block(-1, step)
            far = flag(1, r, e)
            close = flag(0, r, e) & (1 - far)
            low = step < word
            bit = jnp.where(low, step, step - word)
            far_bit, near_bit = far << bit, close << bit
            return (far_low | jnp.where(low, far_bit, 0), far_high | jnp.where(low, 0, far_bit),
                    near_low | jnp.where(low, near_bit, 0), near_high | jnp.where(low, 0, near_bit),
                    count + far + close)

        zero = jnp.int32(0)
        *words, count = lax.fori_loop(0, blocks, gather, (zero,) * 5)
        lead = jnp.maximum(count, LEAD)

        def arrange(s, carry):
            lowest, found, done = [], zero, jnp.bool_(False)
            rest = []
            for n, bits in enumerate(carry):
                take = jnp.logical_and(bits != 0, jnp.logical_not(done))
                one = bits & -bits
                index = zero
                for level in range(5):
                    pattern = sum(1 << b for b in range(word) if (b >> level) & 1)
                    index = index + jnp.where((one & pattern) != 0, 1 << level, 0)
                found = jnp.where(take, index + (n % 2) * word, found)
                rest.append(jnp.where(take, bits ^ one, bits))
                done = jnp.logical_or(done, take)
            order[d * STREAM + s] = jnp.where(s < lead, unit_base[d] + found, stream_base[d] + s - lead)
            return tuple(rest)

        lax.fori_loop(0, STREAM, arrange, tuple(words))

        def far_count(step, carry):
            r, e = of_block(-2, step)
            return carry + flag(3, r, e)

        far_total = lax.fori_loop(0, blocks, far_count, zero)

        def second(step, carry):
            far_seen, near_seen = carry
            r, e = of_block(-2, step)
            far = flag(3, r, e)
            close = flag(2, r, e) & (1 - far)
            spot = jnp.where(far == 1, far_seen, far_total + near_seen)
            slot_of[(HOPS - 2 * sign) * blocks + step] = stream_base[d] + jnp.minimum(spot, STREAM - 1)
            return far_seen + far, near_seen + close

        far_seen, near_seen = lax.fori_loop(0, blocks, second, (zero, zero))
        start = jnp.maximum(far_seen + near_seen, LEAD)

        def third(step, carry):
            r, e = of_block(-3, step)
            slot_of[(HOPS - 3 * sign) * blocks + step] = stream_base[d] + jnp.minimum(start + carry, STREAM - 1)
            return carry + flag(4, r, e)

        lax.fori_loop(0, blocks, third, zero)

        @pl.loop(0, blocks)
        def _(step):
            slot_of[(HOPS - sign) * blocks + step] = unit_base[d] + step

    @pl.loop(0, blocks)
    def _(step):
        slot_of[HOPS * blocks + step] = step

    def find(step):
        t, k = step // slots, lax.rem(step, slots)
        i = first_row + t
        j = table[k, i]
        base = jnp.minimum(wrapped(j - first_row + HOPS * rows_here), units * rows_here - 1) * slots
        there = [table[s, j] for s in range(slots)]
        for m in range(slots):
            wanted = table[m, i]
            found = jnp.int32(-1)
            for s in range(slots):
                found = jnp.where(there[s] == wanted, s, found)
            spot = slot_of[base + jnp.maximum(found, 0)]
            place[step * slots + m] = jnp.where(found < 0, empty, spot)

    own_copy.wait()
    for t in range(rows_here):
        for k in range(slots):
            block = mine[t * slots + k]
            turned = jnp.concatenate([block[:, width // 2:], block[:, :width // 2]], axis=1)
            left_side[t, :, k * width:(k + 1) * width] = jnp.where(layer == 0, block, turned)

    for r in range(rows_here):
        for d in range(2):
            unit_copy(d, r).wait_recv()
            unit_across(d, r).start()

    def take(d, c):
        stream_copy(d, c).wait_recv()
        stream_across(d, c).start()
        mine[pl.ds(stream_base[d] + c * CHUNK, CHUNK)] = landed[d, pl.ds(c * CHUNK, CHUNK)]

    for c in range(chunks):
        for d in range(2):
            if c * CHUNK >= LEAD:
                take(d, c - LEAD // CHUNK)
            for s in range(c * CHUNK, (c + 1) * CHUNK):
                packed[d, s] = mine[order[d * STREAM + s]]
            stream_copy(d, c).start()
        if c < chunks - 1:
            pl.loop(c * blocks // (chunks - 1), (c + 1) * blocks // (chunks - 1))(find)
        if c == chunks - 1:
            rows_copy.wait()
            longest_ref[0, 0] = stream_lengths(table_rows, total_rows, rows_here)
    for c in range(chunks - LEAD // CHUNK, chunks):
        for d in range(2):
            take(d, c)

    own_across().wait_recv()
    for d in range(2):
        for r in range(rows_here):
            unit_across(d, r).wait_recv()
        for c in range(chunks):
            stream_across(d, c).wait_recv()

    pairs = slots // 2

    @pl.loop(0, rows_here * pairs, unroll=5)
    def _(step):
        t, pair = step // pairs, lax.rem(step, pairs)
        first = t * slots * slots + 2 * pair

        def block(index):
            return jnp.concatenate([mine[index], theirs[index]], axis=0)

        right = jnp.concatenate([
            jnp.concatenate([block(place[first + k * slots]), block(place[first + k * slots + 1])], axis=1)
            for k in range(slots)], axis=0)
        product = jnp.dot(left_side[t], right, preferred_element_type=jnp.float32).astype(out_ref.dtype)
        out_ref[t, 2 * pair] = product[:, :width]
        out_ref[t, 2 * pair + 1] = product[:, width:]

    own_across().wait_send()
    for d in range(2):
        for r in range(rows_here):
            unit_copy(d, r).wait_send()
            unit_across(d, r).wait_send()
        for c in range(chunks):
            stream_copy(d, c).wait_send()
            stream_across(d, c).wait_send()


def sparse_square(sizes, table, values):
    rows_here, slots, half, width = values.shape
    blocks = rows_here * slots
    spots = 3 * blocks + 2 * STREAM + 1
    units = 2 * HOPS + 1
    chunks = STREAM // CHUNK
    crossings = 1 + 2 * rows_here + 2 * chunks
    return pl.pallas_call(
        functools.partial(sparse_kernel, sizes),
        out_shape=[jax.ShapeDtypeStruct(values.shape, values.dtype), jax.ShapeDtypeStruct((1, 1), jnp.int32)],
        in_specs=[pl.BlockSpec(memory_space=pl.ANY), pl.BlockSpec(memory_space=pl.ANY)],
        out_specs=[pl.BlockSpec(memory_space=pltpu.VMEM), pl.BlockSpec(memory_space=pltpu.SMEM)],
        scratch_shapes=[
            pltpu.VMEM((spots, half, width), values.dtype),
            pltpu.VMEM((spots, half, width), values.dtype),
            pltpu.VMEM((2, STREAM, half, width), values.dtype),
            pltpu.VMEM((2, STREAM, half, width), values.dtype),
            pltpu.VMEM((rows_here, half, slots * width), values.dtype),
            pltpu.SMEM(table.shape, jnp.int32),
            pltpu.VMEM(table.shape, jnp.int32),
            pltpu.SMEM((5 * rows_here,), jnp.int32),
            pltpu.SMEM((10 * rows_here,), jnp.int32),
            pltpu.SMEM((2 * STREAM,), jnp.int32),
            pltpu.SMEM((units * blocks,), jnp.int32),
            pltpu.SMEM((blocks * slots,), jnp.int32),
            pltpu.SemaphoreType.DMA((2, rows_here)),
            pltpu.SemaphoreType.DMA((2, rows_here)),
            pltpu.SemaphoreType.DMA((2, chunks)),
            pltpu.SemaphoreType.DMA((2, chunks)),
            pltpu.SemaphoreType.DMA((crossings,)),
            pltpu.SemaphoreType.DMA((crossings,)),
            pltpu.SemaphoreType.DMA((3,)),
        ],
        compiler_params=pltpu.CompilerParams(
            collective_id=0, has_side_effects=True, vmem_limit_bytes=56 << 20),
        name="sparse_square",
    )(table, values.reshape(blocks, half, width))


def on_device(sizes, values, columns):
    table = columns.T
    square, longest = sparse_square(sizes, table, values)
    return lax.cond(longest[0, 0] > STREAM,
                    lambda: whole_square(sizes, table, values),
                    lambda: square)


def solution(mesh):
    return jax.shard_map(
        functools.partial(on_device, (mesh.shape["row"], mesh.shape["col"])),
        mesh=mesh,
        in_specs=(P(("row", "col"), None, "layer", None), P()),
        out_specs=P(("row", "col"), None, "layer", None),
        check_vma=False,
    )
```

```python
import functools

import jax
import jax.numpy as jnp
from jax import lax
from jax.experimental import pallas as pl
from jax.experimental.pallas import tpu as pltpu
from jax.sharding import PartitionSpec as P

HOPS = 3
REACH = 12
SPAN = 2 * REACH
STREAM = 92
SEAM_STREAM = 84
CHUNK = 4
LAG = 5
FIRST_LAG = 3
MESH = pl.DeviceIdType.MESH


def whole_kernel(sizes, columns_ref, values_ref, out_ref, near, own, table, place,
                 hop_send, hop_recv, core_send, core_recv, local_sem):
    rows_axis, cols_axis = sizes
    positions = rows_axis * cols_axis
    rows_here, slots, half, width = values_ref.shape
    total_rows = rows_here * positions
    row, col, layer = lax.axis_index("row"), lax.axis_index("col"), lax.axis_index("layer")
    position = row * cols_axis + col
    units = 2 * HOPS + 1
    empty = units * rows_here * slots

    def at(offset):
        there = lax.rem(position + offset + positions, positions)
        return (there // cols_axis, lax.rem(there, cols_axis), layer)

    sibling = (row, col, 1 - layer)
    my_half = pl.ds(pl.multiple_of(layer * half, half), half)

    def unit_rows(unit, r):
        return near.at[pl.ds((unit * rows_here + r) * slots, slots), my_half, :]

    def hop(h, direction, r):
        index = 0 if direction > 0 else 1
        source = values_ref.at[r] if h == 0 else unit_rows(HOPS - direction * h, r)
        return pltpu.make_async_remote_copy(
            source, unit_rows(HOPS - direction * (h + 1), r),
            hop_send.at[h, index, r], hop_recv.at[h, index, r],
            device_id=at(direction), device_id_type=MESH)

    def across(unit, r):
        source = values_ref.at[r] if unit == HOPS else unit_rows(unit, r)
        return pltpu.make_async_remote_copy(
            source, unit_rows(unit, r), core_send.at[unit, r], core_recv.at[unit, r],
            device_id=sibling, device_id_type=MESH)

    table_copy = pltpu.make_async_copy(columns_ref, table, local_sem.at[0])
    own_copy = pltpu.make_async_copy(values_ref, own, local_sem.at[1])
    table_copy.start()
    own_copy.start()

    barrier = pltpu.get_barrier_semaphore()
    for peer in (at(1), at(-1), sibling):
        pl.semaphore_signal(barrier, inc=1, device_id=peer, device_id_type=MESH)
    pl.semaphore_wait(barrier, 3)

    for r in range(rows_here):
        for direction in (1, -1):
            hop(0, direction, r).start()
    for r in range(rows_here):
        across(HOPS, r).start()
    near[empty] = jnp.zeros((2 * half, width), near.dtype)
    near_own = [pltpu.make_async_copy(values_ref.at[r], unit_rows(HOPS, r), local_sem.at[2 + r]) for r in range(rows_here)]
    for copy in near_own:
        copy.start()
    table_copy.wait()

    @pl.loop(0, rows_here * slots)
    def _(step):
        t, k = step // slots, lax.rem(step, slots)
        i = position * rows_here + t
        j = table[k, i]
        base = lax.rem(j - position * rows_here + HOPS * rows_here + total_rows, total_rows) * slots
        there = [table[s, j] for s in range(slots)]
        for m in range(slots):
            wanted = table[m, i]
            found = empty
            for s in range(slots):
                found = jnp.where(there[s] == wanted, base + s, found)
            place[step * slots + m] = jnp.minimum(found, empty)

    for h in range(HOPS):
        for r in range(rows_here):
            for direction in (1, -1):
                hop(h, direction, r).wait_recv()
                if h + 1 < HOPS:
                    hop(h + 1, direction, r).start()
                across(HOPS - direction * (h + 1), r).start()
    own_copy.wait()
    for copy in near_own:
        copy.wait()
    for unit in range(units):
        for r in range(rows_here):
            across(unit, r).wait_recv()

    pairs = slots // 2

    @pl.loop(0, rows_here * pairs)
    def _(step):
        t, pair = step // pairs, lax.rem(step, pairs)
        left = jnp.concatenate([own[t, k] for k in range(slots)], axis=1)
        first = t * slots * slots + 2 * pair
        right = jnp.concatenate([
            jnp.concatenate([near[place[first + k * slots]], near[place[first + k * slots + 1]]], axis=1)
            for k in range(slots)], axis=0)
        product = jnp.dot(left, right, preferred_element_type=jnp.float32).astype(out_ref.dtype)
        out_ref[t, 2 * pair] = product[:, :width]
        out_ref[t, 2 * pair + 1] = product[:, width:]

    for h in range(HOPS):
        for r in range(rows_here):
            for direction in (1, -1):
                hop(h, direction, r).wait_send()
    for unit in range(units):
        for r in range(rows_here):
            across(unit, r).wait_send()


def whole_square(sizes, table, values):
    rows_here, slots, half, width = values.shape
    units = 2 * HOPS + 1
    return pl.pallas_call(
        functools.partial(whole_kernel, sizes),
        out_shape=jax.ShapeDtypeStruct(values.shape, values.dtype),
        in_specs=[pl.BlockSpec(memory_space=pl.ANY), pl.BlockSpec(memory_space=pl.ANY)],
        out_specs=pl.BlockSpec(memory_space=pltpu.VMEM),
        scratch_shapes=[
            pltpu.VMEM((units * rows_here * slots + 1, 2 * half, width), values.dtype),
            pltpu.VMEM(values.shape, values.dtype),
            pltpu.SMEM(table.shape, jnp.int32),
            pltpu.SMEM((rows_here * slots * slots,), jnp.int32),
            pltpu.SemaphoreType.DMA((HOPS, 2, rows_here)),
            pltpu.SemaphoreType.DMA((HOPS, 2, rows_here)),
            pltpu.SemaphoreType.DMA((units, rows_here)),
            pltpu.SemaphoreType.DMA((units, rows_here)),
            pltpu.SemaphoreType.DMA((2 + rows_here,)),
        ],
        compiler_params=pltpu.CompilerParams(
            collective_id=1, has_side_effects=True, vmem_limit_bytes=56 << 20),
        name="whole_square",
    )(table, values)


def shifted_mask(mask, step):
    return mask << -step if step < 0 else mask >> step


def seam_streams(col, cols_axis):
    return (col >= cols_axis - 1) | (col <= 1)


def layout(first, tail, far_first, far_tail, last_first, last_tail, behind, larger):
    lead = LAG * CHUNK

    def starts(n):
        one = larger(first + behind(tail, n), first + FIRST_LAG * CHUNK)
        two = larger(one + behind(far_first, n + 1),
                     first + behind(tail, n + 1) - behind(last_tail, n + 1) + lead)
        return one, two

    one, two = starts(0)
    one_behind, two_behind = starts(1)
    three = larger(two + behind(far_tail, 1), one_behind + lead)
    four = larger(three + behind(last_first, 2), two_behind + lead)
    return one, two, three, four, four + behind(last_tail, 2)


def stream_excess(table_ref, total_rows, rows_here, cols_axis):
    table = table_ref[...]
    slots = table.shape[0]
    lane = lax.broadcasted_iota(jnp.int32, table.shape, 1)
    place = (table - lane + REACH) & 31
    masks = jnp.sum(jnp.left_shift(jnp.ones_like(place), place), axis=0, keepdims=True)
    masks = jnp.broadcast_to(masks, (8, total_rows))
    own_row_index = lax.broadcasted_iota(jnp.int32, masks.shape, 1)
    own_row = own_row_index % rows_here

    def ahead(array, steps):
        return pltpu.roll(array, (-steps) % total_rows, 1)

    seam = seam_streams((own_row_index // rows_here) % cols_axis, cols_axis)
    most = jnp.full((1, total_rows), -STREAM, jnp.int32)
    for direction in (1, -1):
        wanted = {}
        for away in range(1, HOPS + 1):
            got = jnp.zeros_like(masks)
            for step in range(away * rows_here - rows_here + 1, away * rows_here + rows_here):
                if step > REACH:
                    continue
                step = direction * step
                there = ahead(masks, step)
                row_there = own_row + step - direction * away * rows_here
                use = (row_there >= 0) & (row_there < rows_here)
                use = use & (((there >> (REACH - step)) & 1) == 1)
                got = got | jnp.where(use, shifted_mask(there, -step), 0)
            wanted[away] = got[0:1]
        own_first = (own_row >= rows_here // 2) if direction > 0 else (own_row < rows_here // 2)

        def counts(mask):
            hits = jnp.sum((jnp.broadcast_to(mask, place.shape) >> place) & 1, axis=0, keepdims=True)
            hits = jnp.broadcast_to(hits, (8, total_rows))
            totals = []
            for part in (jnp.where(own_first, hits, 0), jnp.where(own_first, 0, hits)):
                summed = part
                for r in range(1, rows_here):
                    summed = summed + ahead(part, r)
                totals.append(summed)
            return totals

        _, tail = counts(wanted[1] | wanted[2] | wanted[3])
        far_first, far_tail = counts(wanted[2] | wanted[3])
        last_first, last_tail = counts(wanted[3])
        end = layout(rows_here // 2 * slots, tail, far_first, far_tail, last_first, last_tail,
                     lambda count, n: ahead(count, -direction * rows_here * n), jnp.maximum)[-1]
        room = jnp.where(seam, SEAM_STREAM, STREAM) if direction > 0 else STREAM
        most = jnp.maximum(most, jnp.where(own_row == 0, end - room, -STREAM)[0:1])
    return jnp.max(most)


def ones(bits):
    bits = bits - ((bits >> 1) & 0x55555555)
    bits = (bits & 0x33333333) + ((bits >> 2) & 0x33333333)
    bits = (bits + (bits >> 4)) & 0x0F0F0F0F
    return (bits * 0x01010101) >> 24


def lowest(bits, limit):
    one = bits & -bits
    index = jnp.int32(0)
    for level in range(5):
        pattern = sum(1 << b for b in range(limit) if (b >> level) & 1)
        index = index + jnp.where((one & pattern) != 0, 1 << level, 0)
    return index, bits ^ one


def sparse_kernel(sizes, columns_ref, values_ref, out_ref, excess_ref, own, mine, theirs, landed, packed, left_side,
                  table, table_rows, masks, needs, order, slot_of, place,
                  unit_send, unit_recv, stream_send, stream_recv, core_send, core_recv, local_sem):
    rows_axis, cols_axis = sizes
    positions = rows_axis * cols_axis
    blocks, half, width = values_ref.shape
    rows_here, slots = out_ref.shape[:2]
    total_rows = rows_here * positions
    row, col, layer = lax.axis_index("row"), lax.axis_index("col"), lax.axis_index("layer")
    position = row * cols_axis + col
    first_row = position * rows_here
    first_rows = rows_here // 2
    first = first_rows * slots
    chunks = (STREAM - first) // CHUNK
    directions = (1, -1)
    stream_base = (blocks, blocks + STREAM)
    empty = blocks + 2 * STREAM
    units = 2 * HOPS + 1

    def at(offset):
        there = lax.rem(position + offset + positions, positions)
        return (there // cols_axis, lax.rem(there, cols_axis), layer)

    sibling = (row, col, 1 - layer)

    def row_of(d, n):
        return rows_here - 1 - n if d == 0 else n

    def unit_copy(d, n):
        return pltpu.make_async_remote_copy(
            values_ref.at[pl.ds(row_of(d, n) * slots, slots)], mine.at[pl.ds(stream_base[d] + n * slots, slots)],
            unit_send.at[d, n], unit_recv.at[d, n], device_id=at(directions[d]), device_id_type=MESH)

    def stream_copy(d, c):
        part = pl.ds(c * CHUNK, CHUNK)
        return pltpu.make_async_remote_copy(
            packed.at[d, part], landed.at[d, part], stream_send.at[d, c], stream_recv.at[d, c],
            device_id=at(directions[d]), device_id_type=MESH)

    def own_across():
        return pltpu.make_async_remote_copy(
            values_ref, theirs.at[pl.ds(0, blocks)], core_send.at[0], core_recv.at[0],
            device_id=sibling, device_id_type=MESH)

    def unit_across(d, n):
        part = pl.ds(stream_base[d] + n * slots, slots)
        index = 1 + d * first_rows + n
        return pltpu.make_async_remote_copy(
            mine.at[part], theirs.at[part], core_send.at[index], core_recv.at[index],
            device_id=sibling, device_id_type=MESH)

    def stream_across(d, c):
        index = 1 + 2 * first_rows + d * chunks + c
        return pltpu.make_async_remote_copy(
            landed.at[d, pl.ds(c * CHUNK, CHUNK)], theirs.at[pl.ds(stream_base[d] + first + c * CHUNK, CHUNK)],
            core_send.at[index], core_recv.at[index], device_id=sibling, device_id_type=MESH)

    table_copy = pltpu.make_async_copy(columns_ref, table, local_sem.at[0])
    rows_copy = pltpu.make_async_copy(columns_ref, table_rows, local_sem.at[1])
    own_copy = pltpu.make_async_copy(values_ref, own, local_sem.at[2])
    mine_copy = pltpu.make_async_copy(values_ref, mine.at[pl.ds(0, blocks)], local_sem.at[3])
    table_copy.start()
    rows_copy.start()
    own_copy.start()
    mine_copy.start()

    barrier = pltpu.get_barrier_semaphore()
    for peer in (at(1), at(-1), sibling):
        pl.semaphore_signal(barrier, inc=1, device_id=peer, device_id_type=MESH)
    pl.semaphore_wait(barrier, 3)

    for n in range(first_rows):
        for d in range(2):
            unit_copy(d, n).start()
    own_across().start()
    mine[empty] = jnp.zeros((half, width), mine.dtype)
    theirs[empty] = jnp.zeros((half, width), mine.dtype)

    table_copy.wait()
    zero = jnp.int32(0)

    def wrapped(value):
        value = jnp.where(value < 0, value + total_rows, value)
        return jnp.where(value >= total_rows, value - total_rows, value)

    def distance(entry, i):
        return (entry - i + REACH) & 31

    @pl.loop(0, units * rows_here)
    def _(n):
        i = wrapped(first_row - HOPS * rows_here + n)
        mask = zero
        for k in range(slots):
            mask = mask | (jnp.int32(1) << distance(table[k, i], i))
        masks[n] = mask

    def unit_mask(unit, r):
        return masks[rows_here * (unit + HOPS) + r]

    def need(source, receiver, r):
        got = zero
        for t in range(rows_here):
            step = rows_here * (source - receiver) + r - t
            if abs(step) <= REACH:
                mask = unit_mask(receiver, t)
                got = got | jnp.where(((mask >> (step + REACH)) & 1) == 1, shifted_mask(mask, step), 0)
        return got

    def needs_at(d, back, n, which):
        return ((d * (HOPS + 1) + back) * rows_here + n) * 3 + which

    def fill_needs(d, back):
        sign = directions[d]
        for n in range(rows_here):
            r = row_of(d, n)
            near, far, last = (need(-sign * back, sign * (away - back), r) for away in (1, 2, 3))
            for which, bits in enumerate((near | far | last, far | last, last)):
                needs[needs_at(d, back, n, which)] = bits

    def of_row(d, back, n):
        r = row_of(d, n)
        j = wrapped(first_row - directions[d] * back * rows_here + r)
        wanted = [needs[needs_at(d, back, n, which)] for which in range(3)]
        blocks_here = []
        for s in range(slots):
            e = distance(table[s, j], j)
            blocks_here.append((r * slots + s, *((bits >> e) & 1 for bits in wanted)))
        return blocks_here

    def count(d, back, which, rows):
        total = zero
        for n in rows:
            bits = needs[needs_at(d, back, n, which)] & unit_mask(-directions[d] * back, row_of(d, n))
            total = total + ones(bits)
        return total

    firsts, tails = range(first_rows), range(first_rows, rows_here)

    for d in range(2):
        fill_needs(d, 0)

        bits = zero
        for n in tails:
            for s, (_, near, _, _) in enumerate(of_row(d, 0, n)):
                bits = bits | (near << ((n - first_rows) * slots + s))

        def natural(found):
            n = found // slots if d == 1 else 1 - found // slots
            base = first if d == 1 else 0
            return base + n * slots + lax.rem(found, slots)

        def arrange(s, bits):
            found, bits = lowest(bits, blocks - first)
            order[d * STREAM + s] = natural(found)
            return bits

        lax.fori_loop(first, blocks, arrange, bits)

    own_copy.wait()

    sends_short = seam_streams(col, cols_axis)
    gets_short = seam_streams(lax.rem(col + cols_axis - 1, cols_axis), cols_axis)

    def unless(short, d, c, step):
        if d == 0 and first + c * CHUNK >= SEAM_STREAM:
            pl.when(jnp.logical_not(short))(step)
        else:
            step()

    def pack(d, c, source):
        def step():
            for s in range(c * CHUNK, (c + 1) * CHUNK):
                packed[d, s] = source[order[d * STREAM + first + s]]
            stream_copy(d, c).start()
        unless(sends_short, d, c, step)

    for c in range(FIRST_LAG):
        for d in range(2):
            pack(d, c, own)

    for d, sign in enumerate(directions):
        for back in range(1, HOPS + 1):
            fill_needs(d, back)
        tail = [count(d, back, 0, tails) for back in range(HOPS + 1)]
        far_first, far_tail = ([count(d, back, 1, rows) for back in range(HOPS + 1)] for rows in (firsts, tails))
        last_first, last_tail = ([count(d, back, 2, rows) for back in range(HOPS + 1)] for rows in (firsts, tails))

        def starts(here):
            return layout(first, tail, far_first, far_tail, last_first, last_tail,
                          lambda counts, n: counts[min(here + n, HOPS)], jnp.maximum)

        one, two, three, four, _ = starts(0)
        one_in, two_in, three_in, four_in, _ = starts(1)
        base = stream_base[d]

        def note(back, block, spot):
            slot_of[(HOPS - sign * back) * blocks + block] = base + jnp.clip(spot, 0, STREAM - 1)

        words = []
        seen = zero
        for rows in (firsts, tails):
            last_bits = far_bits = zero
            for n in rows:
                for s, (block, near, far, last) in enumerate(of_row(d, 1, n)):
                    step = (n - rows[0]) * slots + s
                    last_bits = last_bits | (last << step)
                    far_bits = far_bits | ((far & (1 - last)) << step)
                    if rows is firsts:
                        note(1, block, step)
                    else:
                        note(1, block, first + seen)
                        seen = seen + near
            words += [last_bits, far_bits]

        for rows, start, total, later in ((firsts, one_in, last_first[2], three_in), (tails, two_in, last_tail[2], four_in)):
            last_spot, far_spot, spot = start, start + total, later
            for n in rows:
                for block, _, far, last in of_row(d, 2, n):
                    note(2, block, jnp.where(last == 1, last_spot, far_spot))
                    last_spot = last_spot + last
                    far_spot = far_spot + (far & (1 - last))
                for block, _, _, last in of_row(d, 3, n):
                    note(3, block, spot)
                    spot = spot + last

        def arrange(with_own, s, carry):
            bits_one, bits_two, bits_three, bits_four = carry
            from_first = s < two
            use_last = jnp.where(from_first, bits_one, bits_three) != 0
            bits = jnp.where(from_first, jnp.where(use_last, bits_one, bits_two),
                             jnp.where(use_last, bits_three, bits_four))
            found, rest = lowest(bits, first)
            n, r = found // slots, lax.rem(found, slots)
            n = jnp.where(from_first, n, first_rows + n)
            spot = slot_of[(HOPS - sign) * blocks + (rows_here - 1 - n if d == 0 else n) * slots + r]
            spot = jnp.where(s >= three, base + one_in + s - three, spot)
            spot = jnp.where(s >= four, base + two_in + s - four, spot)
            spot = jnp.clip(spot, 0, empty)
            active = True
            if with_own:
                active = s >= one
                spot = jnp.where(active, spot, order[d * STREAM + s])
            order[d * STREAM + s] = spot
            pick = [from_first & use_last, from_first & ~use_last, ~from_first & use_last, ~from_first & ~use_last]
            return tuple(jnp.where(p & active, rest, b) for p, b in zip(pick, carry))

        carry = lax.fori_loop(first + FIRST_LAG * CHUNK, blocks, functools.partial(arrange, True), tuple(words))
        lax.fori_loop(blocks, STREAM, functools.partial(arrange, False), carry)

    @pl.loop(0, blocks)
    def _(step):
        slot_of[HOPS * blocks + step] = step

    def find(step):
        t, k = step // slots, lax.rem(step, slots)
        i = first_row + t
        j = table[k, i]
        base = jnp.minimum(wrapped(j - first_row + HOPS * rows_here), units * rows_here - 1) * slots
        there = [table[s, j] for s in range(slots)]
        for m in range(slots):
            wanted = table[m, i]
            found = jnp.int32(-1)
            for s in range(slots):
                found = jnp.where(there[s] == wanted, s, found)
            spot = slot_of[base + jnp.maximum(found, 0)]
            place[step * slots + m] = jnp.where(found < 0, empty, spot)

    def take(d, c):
        def step():
            stream_copy(d, c).wait_recv()
            stream_across(d, c).start()
            mine[pl.ds(stream_base[d] + first + c * CHUNK, CHUNK)] = landed[d, pl.ds(c * CHUNK, CHUNK)]
        unless(gets_short, d, c, step)

    mine_copy.wait()
    for n in range(first_rows):
        for d in range(2):
            unit_copy(d, n).wait_recv()
            unit_across(d, n).start()

    shares = 10
    for c in range(FIRST_LAG, chunks):
        for d in range(2):
            if c >= LAG:
                take(d, c - LAG)
            pack(d, c, mine)
        n = c - FIRST_LAG
        if n < shares:
            pl.loop(n * blocks // shares, (n + 1) * blocks // shares)(find)
    rows_copy.wait()
    excess_ref[0, 0] = stream_excess(table_rows, total_rows, rows_here, cols_axis)
    for t in range(rows_here):
        for k in range(slots):
            block = own[t * slots + k]
            turned = jnp.concatenate([block[:, width // 2:], block[:, :width // 2]], axis=1)
            left_side[t, :, k * width:(k + 1) * width] = jnp.where(layer == 0, block, turned)
    for c in range(chunks - LAG, chunks):
        for d in range(2):
            take(d, c)

    own_across().wait_recv()
    for d in range(2):
        for n in range(first_rows):
            unit_across(d, n).wait_recv()
        for c in range(chunks):
            unless(gets_short, d, c, lambda d=d, c=c: stream_across(d, c).wait_recv())

    pairs = slots // 2

    @pl.loop(0, rows_here * pairs, unroll=5)
    def _(step):
        t, pair = step // pairs, lax.rem(step, pairs)
        start = t * slots * slots + 2 * pair

        def block(index):
            return jnp.concatenate([mine[index], theirs[index]], axis=0)

        right = jnp.concatenate([
            jnp.concatenate([block(place[start + k * slots]), block(place[start + k * slots + 1])], axis=1)
            for k in range(slots)], axis=0)
        product = jnp.dot(left_side[t], right, preferred_element_type=jnp.float32).astype(out_ref.dtype)
        out_ref[t, 2 * pair] = product[:, :width]
        out_ref[t, 2 * pair + 1] = product[:, width:]

    own_across().wait_send()
    for d in range(2):
        for n in range(first_rows):
            unit_copy(d, n).wait_send()
            unit_across(d, n).wait_send()
        for c in range(chunks):
            unless(sends_short, d, c, lambda d=d, c=c: stream_copy(d, c).wait_send())
            unless(gets_short, d, c, lambda d=d, c=c: stream_across(d, c).wait_send())


def sparse_square(sizes, table, values):
    rows_here, slots, half, width = values.shape
    blocks = rows_here * slots
    first_rows = rows_here // 2
    spots = blocks + 2 * STREAM + 1
    units = 2 * HOPS + 1
    chunks = (STREAM - first_rows * slots) // CHUNK
    crossings = 1 + 2 * first_rows + 2 * chunks
    return pl.pallas_call(
        functools.partial(sparse_kernel, sizes),
        out_shape=[jax.ShapeDtypeStruct(values.shape, values.dtype), jax.ShapeDtypeStruct((1, 1), jnp.int32)],
        in_specs=[pl.BlockSpec(memory_space=pl.ANY), pl.BlockSpec(memory_space=pl.ANY)],
        out_specs=[pl.BlockSpec(memory_space=pltpu.VMEM), pl.BlockSpec(memory_space=pltpu.SMEM)],
        scratch_shapes=[
            pltpu.VMEM((blocks, half, width), values.dtype),
            pltpu.VMEM((spots, half, width), values.dtype),
            pltpu.VMEM((spots, half, width), values.dtype),
            pltpu.VMEM((2, chunks * CHUNK, half, width), values.dtype),
            pltpu.VMEM((2, chunks * CHUNK, half, width), values.dtype),
            pltpu.VMEM((rows_here, half, slots * width), values.dtype),
            pltpu.SMEM(table.shape, jnp.int32),
            pltpu.VMEM(table.shape, jnp.int32),
            pltpu.SMEM((units * rows_here,), jnp.int32),
            pltpu.SMEM((2 * (HOPS + 1) * rows_here * 3,), jnp.int32),
            pltpu.SMEM((2 * STREAM,), jnp.int32),
            pltpu.SMEM((units * blocks,), jnp.int32),
            pltpu.SMEM((blocks * slots,), jnp.int32),
            pltpu.SemaphoreType.DMA((2, first_rows)),
            pltpu.SemaphoreType.DMA((2, first_rows)),
            pltpu.SemaphoreType.DMA((2, chunks)),
            pltpu.SemaphoreType.DMA((2, chunks)),
            pltpu.SemaphoreType.DMA((crossings,)),
            pltpu.SemaphoreType.DMA((crossings,)),
            pltpu.SemaphoreType.DMA((4,)),
        ],
        compiler_params=pltpu.CompilerParams(
            collective_id=0, has_side_effects=True, vmem_limit_bytes=56 << 20),
        name="sparse_square",
    )(table, values.reshape(blocks, half, width))


def on_device(sizes, values, columns):
    table = columns.T
    square, excess = sparse_square(sizes, table, values)
    return lax.cond(excess[0, 0] > 0,
                    lambda: whole_square(sizes, table, values),
                    lambda: square)


def solution(mesh):
    return jax.shard_map(
        functools.partial(on_device, (mesh.shape["row"], mesh.shape["col"])),
        mesh=mesh,
        in_specs=(P(("row", "col"), None, "layer", None), P()),
        out_specs=P(("row", "col"), None, "layer", None),
        check_vma=False,
    )
```

```python
import functools

import jax
import jax.numpy as jnp
from jax import lax
from jax.experimental import pallas as pl
from jax.experimental.pallas import tpu as pltpu
from jax.sharding import PartitionSpec as P

HOPS = 3
REACH = 12
SPAN = 2 * REACH
STREAM = 92
SEAM_STREAM = 78
CHUNK = 2
LAG = 7
FIRST_LAG = 6
MESH = pl.DeviceIdType.MESH


def whole_kernel(sizes, columns_ref, values_ref, out_ref, near, own, table, place,
                 hop_send, hop_recv, core_send, core_recv, local_sem):
    rows_axis, cols_axis = sizes
    positions = rows_axis * cols_axis
    rows_here, slots, half, width = values_ref.shape
    total_rows = rows_here * positions
    row, col, layer = lax.axis_index("row"), lax.axis_index("col"), lax.axis_index("layer")
    position = row * cols_axis + col
    units = 2 * HOPS + 1
    empty = units * rows_here * slots

    def at(offset):
        there = lax.rem(position + offset + positions, positions)
        return (there // cols_axis, lax.rem(there, cols_axis), layer)

    sibling = (row, col, 1 - layer)
    my_half = pl.ds(pl.multiple_of(layer * half, half), half)

    def unit_rows(unit, r):
        return near.at[pl.ds((unit * rows_here + r) * slots, slots), my_half, :]

    def hop(h, direction, r):
        index = 0 if direction > 0 else 1
        source = values_ref.at[r] if h == 0 else unit_rows(HOPS - direction * h, r)
        return pltpu.make_async_remote_copy(
            source, unit_rows(HOPS - direction * (h + 1), r),
            hop_send.at[h, index, r], hop_recv.at[h, index, r],
            device_id=at(direction), device_id_type=MESH)

    def across(unit, r):
        source = values_ref.at[r] if unit == HOPS else unit_rows(unit, r)
        return pltpu.make_async_remote_copy(
            source, unit_rows(unit, r), core_send.at[unit, r], core_recv.at[unit, r],
            device_id=sibling, device_id_type=MESH)

    table_copy = pltpu.make_async_copy(columns_ref, table, local_sem.at[0])
    own_copy = pltpu.make_async_copy(values_ref, own, local_sem.at[1])
    table_copy.start()
    own_copy.start()

    barrier = pltpu.get_barrier_semaphore()
    for peer in (at(1), at(-1), sibling):
        pl.semaphore_signal(barrier, inc=1, device_id=peer, device_id_type=MESH)
    pl.semaphore_wait(barrier, 3)

    for r in range(rows_here):
        for direction in (1, -1):
            hop(0, direction, r).start()
    for r in range(rows_here):
        across(HOPS, r).start()
    near[empty] = jnp.zeros((2 * half, width), near.dtype)
    near_own = [pltpu.make_async_copy(values_ref.at[r], unit_rows(HOPS, r), local_sem.at[2 + r]) for r in range(rows_here)]
    for copy in near_own:
        copy.start()
    table_copy.wait()

    @pl.loop(0, rows_here * slots)
    def _(step):
        t, k = step // slots, lax.rem(step, slots)
        i = position * rows_here + t
        j = table[k, i]
        base = lax.rem(j - position * rows_here + HOPS * rows_here + total_rows, total_rows) * slots
        there = [table[s, j] for s in range(slots)]
        for m in range(slots):
            wanted = table[m, i]
            found = empty
            for s in range(slots):
                found = jnp.where(there[s] == wanted, base + s, found)
            place[step * slots + m] = jnp.minimum(found, empty)

    for h in range(HOPS):
        for r in range(rows_here):
            for direction in (1, -1):
                hop(h, direction, r).wait_recv()
                if h + 1 < HOPS:
                    hop(h + 1, direction, r).start()
                across(HOPS - direction * (h + 1), r).start()
    own_copy.wait()
    for copy in near_own:
        copy.wait()
    for unit in range(units):
        for r in range(rows_here):
            across(unit, r).wait_recv()

    pairs = slots // 2

    @pl.loop(0, rows_here * pairs)
    def _(step):
        t, pair = step // pairs, lax.rem(step, pairs)
        left = jnp.concatenate([own[t, k] for k in range(slots)], axis=1)
        first = t * slots * slots + 2 * pair
        right = jnp.concatenate([
            jnp.concatenate([near[place[first + k * slots]], near[place[first + k * slots + 1]]], axis=1)
            for k in range(slots)], axis=0)
        product = jnp.dot(left, right, preferred_element_type=jnp.float32).astype(out_ref.dtype)
        out_ref[t, 2 * pair] = product[:, :width]
        out_ref[t, 2 * pair + 1] = product[:, width:]

    for h in range(HOPS):
        for r in range(rows_here):
            for direction in (1, -1):
                hop(h, direction, r).wait_send()
    for unit in range(units):
        for r in range(rows_here):
            across(unit, r).wait_send()


def whole_square(sizes, table, values):
    rows_here, slots, half, width = values.shape
    units = 2 * HOPS + 1
    return pl.pallas_call(
        functools.partial(whole_kernel, sizes),
        out_shape=jax.ShapeDtypeStruct(values.shape, values.dtype),
        in_specs=[pl.BlockSpec(memory_space=pl.ANY), pl.BlockSpec(memory_space=pl.ANY)],
        out_specs=pl.BlockSpec(memory_space=pltpu.VMEM),
        scratch_shapes=[
            pltpu.VMEM((units * rows_here * slots + 1, 2 * half, width), values.dtype),
            pltpu.VMEM(values.shape, values.dtype),
            pltpu.SMEM(table.shape, jnp.int32),
            pltpu.SMEM((rows_here * slots * slots,), jnp.int32),
            pltpu.SemaphoreType.DMA((HOPS, 2, rows_here)),
            pltpu.SemaphoreType.DMA((HOPS, 2, rows_here)),
            pltpu.SemaphoreType.DMA((units, rows_here)),
            pltpu.SemaphoreType.DMA((units, rows_here)),
            pltpu.SemaphoreType.DMA((2 + rows_here,)),
        ],
        compiler_params=pltpu.CompilerParams(
            collective_id=1, has_side_effects=True, vmem_limit_bytes=56 << 20),
        name="whole_square",
    )(table, values)


def shifted_mask(mask, step):
    return mask << -step if step < 0 else mask >> step


def seam_streams(col, cols_axis):
    return (col >= cols_axis - 1) | (col <= 1)


def layout(first, tail, far_first, far_tail, last_first, last_tail, behind, larger):
    lead = LAG * CHUNK

    def starts(n):
        one = larger(first + behind(tail, n), first + FIRST_LAG * CHUNK)
        two = larger(one + behind(far_first, n + 1),
                     first + behind(tail, n + 1) - behind(last_tail, n + 1) + lead)
        return one, two

    one, two = starts(0)
    one_behind, two_behind = starts(1)
    three = larger(two + behind(far_tail, 1), one_behind + lead)
    four = larger(three + behind(last_first, 2), two_behind + lead)
    return one, two, three, four, four + behind(last_tail, 2)


def stream_excess(table_ref, total_rows, rows_here, cols_axis):
    table = table_ref[...]
    slots = table.shape[0]
    lane = lax.broadcasted_iota(jnp.int32, table.shape, 1)
    place = (table - lane + REACH) & 31
    masks = jnp.sum(jnp.left_shift(jnp.ones_like(place), place), axis=0, keepdims=True)
    masks = jnp.broadcast_to(masks, (8, total_rows))
    own_row_index = lax.broadcasted_iota(jnp.int32, masks.shape, 1)
    own_row = own_row_index % rows_here

    def ahead(array, steps):
        return pltpu.roll(array, (-steps) % total_rows, 1)

    seam = seam_streams((own_row_index // rows_here) % cols_axis, cols_axis)
    most = jnp.full((1, total_rows), -STREAM, jnp.int32)
    for direction in (1, -1):
        wanted = {}
        for away in range(1, HOPS + 1):
            got = jnp.zeros_like(masks)
            for step in range(away * rows_here - rows_here + 1, away * rows_here + rows_here):
                if step > REACH:
                    continue
                step = direction * step
                there = ahead(masks, step)
                row_there = own_row + step - direction * away * rows_here
                use = (row_there >= 0) & (row_there < rows_here)
                use = use & (((there >> (REACH - step)) & 1) == 1)
                got = got | jnp.where(use, shifted_mask(there, -step), 0)
            wanted[away] = got[0:1]
        own_first = (own_row >= rows_here // 2) if direction > 0 else (own_row < rows_here // 2)

        def counts(mask):
            hits = jnp.sum((jnp.broadcast_to(mask, place.shape) >> place) & 1, axis=0, keepdims=True)
            hits = jnp.broadcast_to(hits, (8, total_rows))
            totals = []
            for part in (jnp.where(own_first, hits, 0), jnp.where(own_first, 0, hits)):
                summed = part
                for r in range(1, rows_here):
                    summed = summed + ahead(part, r)
                totals.append(summed)
            return totals

        _, tail = counts(wanted[1] | wanted[2] | wanted[3])
        far_first, far_tail = counts(wanted[2] | wanted[3])
        last_first, last_tail = counts(wanted[3])
        end = layout(rows_here // 2 * slots, tail, far_first, far_tail, last_first, last_tail,
                     lambda count, n: ahead(count, -direction * rows_here * n), jnp.maximum)[-1]
        room = jnp.where(seam, SEAM_STREAM, STREAM) if direction > 0 else STREAM
        most = jnp.maximum(most, jnp.where(own_row == 0, end - room, -STREAM)[0:1])
    return jnp.max(most)


def ones(bits):
    bits = bits - ((bits >> 1) & 0x55555555)
    bits = (bits & 0x33333333) + ((bits >> 2) & 0x33333333)
    bits = (bits + (bits >> 4)) & 0x0F0F0F0F
    return (bits * 0x01010101) >> 24


def lowest(bits, limit):
    one = bits & -bits
    index = jnp.int32(0)
    for level in range(5):
        pattern = sum(1 << b for b in range(limit) if (b >> level) & 1)
        index = index + jnp.where((one & pattern) != 0, 1 << level, 0)
    return index, bits ^ one


def sparse_kernel(sizes, columns_ref, values_ref, out_ref, excess_ref, rows_own, own, mine, every, landed, packed,
                  table, table_rows, masks, needs, order, slot_of, place,
                  unit_send, unit_recv, stream_send, stream_recv, core_send, core_recv, local_sem):
    rows_axis, cols_axis = sizes
    positions = rows_axis * cols_axis
    blocks, half, width = values_ref.shape
    rows_here, slots = out_ref.shape[:2]
    total_rows = rows_here * positions
    row, col, layer = lax.axis_index("row"), lax.axis_index("col"), lax.axis_index("layer")
    position = row * cols_axis + col
    first_row = position * rows_here
    first_rows = rows_here // 2
    first = first_rows * slots
    chunks = (STREAM - first) // CHUNK
    units = 2 * HOPS + 1
    empty = blocks + 2 * STREAM
    own_frame, other_frame = layer, 1 - layer

    def at(offset):
        there = lax.rem(position + offset + positions, positions)
        return (there // cols_axis, lax.rem(there, cols_axis), layer)

    ahead, behind = at(1 - 2 * layer), at(2 * layer - 1)
    sibling = (row, col, 1 - layer)
    halves = [pl.ds(pl.multiple_of(which * half, half), half) for which in (layer, 1 - layer)]

    def row_of(frame, r):
        return jnp.where(frame == 0, r, rows_here - 1 - r)

    def blocks_of(frame, r):
        return pl.ds(row_of(frame, r) * slots, slots)

    def stream_base(frame):
        return blocks + frame * STREAM

    def unit_copy(n, which):
        r = rows_here - 1 - n
        source = values_ref.at[blocks_of(own_frame, r)] if which == 0 else own.at[blocks_of(own_frame, r), halves[1], :]
        return pltpu.make_async_remote_copy(
            source, mine.at[pl.ds(blocks + n * slots, slots), halves[which], :],
            unit_send.at[n, which], unit_recv.at[n, which], device_id=ahead, device_id_type=MESH)

    def stream_copy(c):
        part = pl.ds(c * CHUNK, CHUNK)
        return pltpu.make_async_remote_copy(
            packed.at[part], landed.at[part], stream_send.at[c], stream_recv.at[c],
            device_id=ahead, device_id_type=MESH)

    def own_across(r):
        part = blocks_of(other_frame, r)
        return pltpu.make_async_remote_copy(
            values_ref.at[part], own.at[part, halves[0], :], core_send.at[r], core_recv.at[r],
            device_id=sibling, device_id_type=MESH)

    def unit_across():
        index = rows_here
        return pltpu.make_async_remote_copy(
            mine.at[pl.ds(blocks, first)], every.at[pl.ds(stream_base(own_frame), first)],
            core_send.at[index], core_recv.at[index], device_id=sibling, device_id_type=MESH)

    def stream_across(c):
        index = rows_here + 1 + c
        return pltpu.make_async_remote_copy(
            landed.at[pl.ds(c * CHUNK, CHUNK)], every.at[pl.ds(stream_base(own_frame) + first + c * CHUNK, CHUNK)],
            core_send.at[index], core_recv.at[index], device_id=sibling, device_id_type=MESH)

    table_copy = pltpu.make_async_copy(columns_ref, table, local_sem.at[0])
    lanes_copy = pltpu.make_async_copy(columns_ref, table_rows, local_sem.at[1])
    rows_copy = pltpu.make_async_copy(values_ref, rows_own, local_sem.at[2])
    own_copy = pltpu.make_async_copy(values_ref, own.at[:, halves[0], :], local_sem.at[3])
    for copy in (table_copy, own_copy, lanes_copy, rows_copy):
        copy.start()

    barrier = pltpu.get_barrier_semaphore()
    for peer in (behind, sibling):
        pl.semaphore_signal(barrier, inc=1, device_id=peer, device_id_type=MESH)
    pl.semaphore_wait(barrier, 2)

    for r in reversed(range(rows_here)):
        own_across(r).start()
    for n in range(first_rows):
        unit_copy(n, 0).start()
    every[empty] = jnp.zeros((2 * half, width), every.dtype)

    table_copy.wait()
    zero = jnp.int32(0)

    def wrapped(value):
        value = jnp.where(value < 0, value + total_rows, value)
        return jnp.where(value >= total_rows, value - total_rows, value)

    def row_at(frame, r):
        return wrapped(first_row + row_of(frame, r))

    def distance(frame, entry, i):
        return (jnp.where(frame == 0, entry - i, i - entry) + REACH) & 31

    def fill_masks(frame):
        @pl.loop(0, units * rows_here)
        def _(n):
            i = row_at(frame, n - HOPS * rows_here)
            mask = zero
            for k in range(slots):
                mask = mask | (jnp.int32(1) << distance(frame, table[k, i], i))
            masks[n] = mask

    def unit_mask(unit, r):
        return masks[rows_here * (unit + HOPS) + r]

    def need(source, receiver, r):
        got = zero
        for t in range(rows_here):
            step = rows_here * (source - receiver) + r - t
            if abs(step) <= REACH:
                mask = unit_mask(receiver, t)
                got = got | jnp.where(((mask >> (step + REACH)) & 1) == 1, shifted_mask(mask, step), 0)
        return got

    def needs_at(back, n, which):
        return (back * rows_here + n) * 3 + which

    def fill_needs(back):
        for n in range(rows_here):
            near, far, last = (need(-back, away - back, rows_here - 1 - n) for away in (1, 2, 3))
            for which, bits in enumerate((near | far | last, far | last, last)):
                needs[needs_at(back, n, which)] = bits

    def of_row(frame, back, n):
        r = rows_here - 1 - n
        j = row_at(frame, r - back * rows_here)
        start = row_of(frame, r) * slots
        wanted = [needs[needs_at(back, n, which)] for which in range(3)]
        found = []
        for s in range(slots):
            e = distance(frame, table[s, j], j)
            found.append((start + s, *((bits >> e) & 1 for bits in wanted)))
        return found

    def count(back, which, rows):
        total = zero
        for n in rows:
            total = total + ones(needs[needs_at(back, n, which)] & unit_mask(-back, rows_here - 1 - n))
        return total

    firsts, tails = range(first_rows), range(first_rows, rows_here)

    def natural(n, s):
        return row_of(own_frame, rows_here - 1 - n) * slots + s

    fill_masks(own_frame)
    fill_needs(0)
    bits = zero
    for n in tails:
        for s, (_, near, _, _) in enumerate(of_row(own_frame, 0, n)):
            bits = bits | (near << ((n - first_rows) * slots + s))

    def arrange_own(s, bits):
        found, bits = lowest(bits, blocks - first)
        order[s] = natural(first_rows + found // slots, lax.rem(found, slots))
        return bits

    lax.fori_loop(first, blocks, arrange_own, bits)

    own_copy.wait()
    for r in reversed(range(rows_here)):
        own_across(r).wait_recv()
        n = rows_here - 1 - r
        if n < first_rows:
            unit_copy(n, 1).start()
    mine_copy = pltpu.make_async_copy(own, mine.at[pl.ds(0, blocks)], local_sem.at[4])
    every_copy = pltpu.make_async_copy(own, every.at[pl.ds(0, blocks)], local_sem.at[5])
    mine_copy.start()
    every_copy.start()

    right = layer == 0
    sends_short = right & seam_streams(col, cols_axis)
    seam_here = seam_streams(lax.rem(col + cols_axis - 1, cols_axis), cols_axis)
    gets_short = right & seam_here
    other_short = jnp.logical_not(right) & seam_here

    def unless(short, c, step):
        if first + c * CHUNK >= SEAM_STREAM:
            pl.when(jnp.logical_not(short))(step)
        else:
            step()

    def pack(c, source):
        def step():
            for s in range(c * CHUNK, (c + 1) * CHUNK):
                packed[s] = source[order[first + s]]
            stream_copy(c).start()
        unless(sends_short, c, step)

    for c in range(FIRST_LAG):
        pack(c, own)

    def fill_slots(frame, with_order):
        for back in range(1, HOPS + 1):
            fill_needs(back)
        tail = [count(back, 0, tails) for back in range(HOPS + 1)]
        far_first, far_tail = ([count(back, 1, rows) for back in range(HOPS + 1)] for rows in (firsts, tails))
        last_first, last_tail = ([count(back, 2, rows) for back in range(HOPS + 1)] for rows in (firsts, tails))

        def starts(here):
            return layout(first, tail, far_first, far_tail, last_first, last_tail,
                          lambda counts, n: counts[min(here + n, HOPS)], jnp.maximum)

        one_in, two_in, three_in, four_in, _ = starts(1)
        base = stream_base(frame)

        def unit_at(back):
            return jnp.where(frame == 0, HOPS - back, HOPS + back) * blocks

        def note(back, block, spot):
            slot_of[unit_at(back) + block] = base + jnp.clip(spot, 0, STREAM - 1)

        words = []
        seen = zero
        for rows in (firsts, tails):
            last_bits = far_bits = zero
            for n in rows:
                for s, (block, near, far, last) in enumerate(of_row(frame, 1, n)):
                    step = (n - rows[0]) * slots + s
                    if with_order:
                        last_bits = last_bits | (last << step)
                        far_bits = far_bits | ((far & (1 - last)) << step)
                    if rows is firsts:
                        note(1, block, step)
                    else:
                        note(1, block, first + seen)
                        seen = seen + near
            words += [last_bits, far_bits]

        for rows, start, total, later in ((firsts, one_in, last_first[2], three_in), (tails, two_in, last_tail[2], four_in)):
            last_spot, far_spot, spot = start, start + total, later
            for n in rows:
                for block, _, far, last in of_row(frame, 2, n):
                    note(2, block, jnp.where(last == 1, last_spot, far_spot))
                    last_spot = last_spot + last
                    far_spot = far_spot + (far & (1 - last))
                for block, _, _, last in of_row(frame, 3, n):
                    note(3, block, spot)
                    spot = spot + last
        if not with_order:
            return

        one, two, three, four, _ = starts(0)
        unit_behind = unit_at(1)

        def arrange(with_own, s, carry):
            bits_one, bits_two, bits_three, bits_four = carry
            from_first = s < two
            use_last = jnp.where(from_first, bits_one, bits_three) != 0
            bits = jnp.where(from_first, jnp.where(use_last, bits_one, bits_two),
                             jnp.where(use_last, bits_three, bits_four))
            found, rest = lowest(bits, first)
            n = jnp.where(from_first, 0, first_rows) + found // slots
            spot = slot_of[unit_behind + natural(n, lax.rem(found, slots))] - base
            spot = jnp.where(s >= three, one_in + s - three, spot)
            spot = jnp.where(s >= four, two_in + s - four, spot)
            spot = blocks + jnp.clip(spot, 0, STREAM - 1)
            active = True
            if with_own:
                active = s >= one
                spot = jnp.where(active, spot, order[s])
            order[s] = spot
            pick = [from_first & use_last, from_first & ~use_last, ~from_first & use_last, ~from_first & ~use_last]
            return tuple(jnp.where(p & active, rest, b) for p, b in zip(pick, carry))

        carry = lax.fori_loop(first + FIRST_LAG * CHUNK, blocks, functools.partial(arrange, True), tuple(words))
        lax.fori_loop(blocks, STREAM, functools.partial(arrange, False), carry)

    fill_slots(own_frame, True)
    fill_masks(other_frame)
    fill_slots(other_frame, False)

    @pl.loop(0, blocks)
    def _(step):
        slot_of[HOPS * blocks + step] = step

    def find(step):
        t, k = step // slots, lax.rem(step, slots)
        i = first_row + t
        j = table[k, i]
        base = jnp.minimum(wrapped(j - first_row + HOPS * rows_here), units * rows_here - 1) * slots
        there = [table[s, j] for s in range(slots)]
        for m in range(slots):
            wanted = table[m, i]
            found = jnp.int32(-1)
            for s in range(slots):
                found = jnp.where(there[s] == wanted, s, found)
            spot = slot_of[base + jnp.maximum(found, 0)]
            place[step * slots + m] = jnp.where(found < 0, empty, spot)

    def take(c):
        def step():
            stream_copy(c).wait_recv()
            stream_across(c).start()
            got = landed[pl.ds(c * CHUNK, CHUNK)]
            mine[pl.ds(blocks + first + c * CHUNK, CHUNK)] = got
            every[pl.ds(stream_base(own_frame) + first + c * CHUNK, CHUNK)] = got
        unless(gets_short, c, step)

    mine_copy.wait()
    for n in range(first_rows):
        for which in range(2):
            unit_copy(n, which).wait_recv()
    unit_across().start()
    unit_every = pltpu.make_async_copy(
        mine.at[pl.ds(blocks, first)], every.at[pl.ds(stream_base(own_frame), first)], local_sem.at[6])
    unit_every.start()

    shares = blocks // CHUNK
    for c in range(FIRST_LAG, chunks):
        if c >= LAG:
            take(c - LAG)
        pack(c, mine)
        n = c - FIRST_LAG
        if n < shares:
            pl.loop(n * blocks // shares, (n + 1) * blocks // shares)(find)
    lanes_copy.wait()
    excess_ref[0, 0] = stream_excess(table_rows, total_rows, rows_here, cols_axis)
    for c in range(chunks - LAG, chunks):
        take(c)

    rows_copy.wait()
    every_copy.wait()
    unit_every.wait()
    unit_across().wait_recv()
    for c in range(chunks):
        unless(other_short, c, lambda c=c: stream_across(c).wait_recv())

    pairs = slots // 2

    @pl.loop(0, rows_here * pairs, unroll=5)
    def _(step):
        t, pair = step // pairs, lax.rem(step, pairs)
        start = t * slots * slots + 2 * pair
        left = jnp.concatenate([rows_own[t * slots + k] for k in range(slots)], axis=1)
        rhs = jnp.concatenate([
            jnp.concatenate([every[place[start + k * slots]], every[place[start + k * slots + 1]]], axis=1)
            for k in range(slots)], axis=0)
        product = jnp.dot(left, rhs, preferred_element_type=jnp.float32).astype(out_ref.dtype)
        out_ref[t, 2 * pair] = product[:, :width]
        out_ref[t, 2 * pair + 1] = product[:, width:]

    for r in range(rows_here):
        own_across(r).wait_send()
    for n in range(first_rows):
        for which in range(2):
            unit_copy(n, which).wait_send()
    unit_across().wait_send()
    for c in range(chunks):
        unless(sends_short, c, lambda c=c: stream_copy(c).wait_send())
        unless(gets_short, c, lambda c=c: stream_across(c).wait_send())


def sparse_square(sizes, table, values):
    rows_here, slots, half, width = values.shape
    blocks = rows_here * slots
    first_rows = rows_here // 2
    units = 2 * HOPS + 1
    chunks = (STREAM - first_rows * slots) // CHUNK
    crossings = rows_here + 1 + chunks

    def whole_blocks(count):
        return pltpu.VMEM((count, 2 * half, width), values.dtype)

    return pl.pallas_call(
        functools.partial(sparse_kernel, sizes),
        out_shape=[jax.ShapeDtypeStruct(values.shape, values.dtype), jax.ShapeDtypeStruct((1, 1), jnp.int32)],
        in_specs=[pl.BlockSpec(memory_space=pl.ANY), pl.BlockSpec(memory_space=pl.ANY)],
        out_specs=[pl.BlockSpec(memory_space=pltpu.VMEM), pl.BlockSpec(memory_space=pltpu.SMEM)],
        scratch_shapes=[
            pltpu.VMEM((blocks, half, width), values.dtype),
            whole_blocks(blocks),
            whole_blocks(blocks + STREAM),
            whole_blocks(blocks + 2 * STREAM + 1),
            whole_blocks(chunks * CHUNK),
            whole_blocks(chunks * CHUNK),
            pltpu.SMEM(table.shape, jnp.int32),
            pltpu.VMEM(table.shape, jnp.int32),
            pltpu.SMEM((units * rows_here,), jnp.int32),
            pltpu.SMEM(((HOPS + 1) * rows_here * 3,), jnp.int32),
            pltpu.SMEM((STREAM,), jnp.int32),
            pltpu.SMEM((units * blocks,), jnp.int32),
            pltpu.SMEM((blocks * slots,), jnp.int32),
            pltpu.SemaphoreType.DMA((first_rows, 2)),
            pltpu.SemaphoreType.DMA((first_rows, 2)),
            pltpu.SemaphoreType.DMA((chunks,)),
            pltpu.SemaphoreType.DMA((chunks,)),
            pltpu.SemaphoreType.DMA((crossings,)),
            pltpu.SemaphoreType.DMA((crossings,)),
            pltpu.SemaphoreType.DMA((7,)),
        ],
        compiler_params=pltpu.CompilerParams(
            collective_id=0, has_side_effects=True, vmem_limit_bytes=56 << 20),
        name="sparse_square",
    )(table, values.reshape(blocks, half, width))


def on_device(sizes, values, columns):
    table = columns.T
    square, excess = sparse_square(sizes, table, values)
    return lax.cond(excess[0, 0] > 0,
                    lambda: whole_square(sizes, table, values),
                    lambda: square)


def solution(mesh):
    return jax.shard_map(
        functools.partial(on_device, (mesh.shape["row"], mesh.shape["col"])),
        mesh=mesh,
        in_specs=(P(("row", "col"), None, "layer", None), P()),
        out_specs=P(("row", "col"), None, "layer", None),
        check_vma=False,
    )
```

```python
import functools

import jax
import jax.numpy as jnp
from jax import lax
from jax.experimental import pallas as pl
from jax.experimental.pallas import tpu as pltpu
from jax.sharding import PartitionSpec as P

HOPS = 3
REACH = 12
SPAN = 2 * REACH
STREAM = 92
SEAM_STREAM = 80
CHUNK = 4
LAG = 4
FIRST_LAG = 3
MESH = pl.DeviceIdType.MESH


def whole_kernel(sizes, columns_ref, values_ref, out_ref, near, own, table, place,
                 hop_send, hop_recv, core_send, core_recv, local_sem):
    rows_axis, cols_axis = sizes
    positions = rows_axis * cols_axis
    rows_here, slots, half, width = values_ref.shape
    total_rows = rows_here * positions
    row, col, layer = lax.axis_index("row"), lax.axis_index("col"), lax.axis_index("layer")
    position = row * cols_axis + col
    units = 2 * HOPS + 1
    empty = units * rows_here * slots

    def at(offset):
        there = lax.rem(position + offset + positions, positions)
        return (there // cols_axis, lax.rem(there, cols_axis), layer)

    sibling = (row, col, 1 - layer)
    my_half = pl.ds(pl.multiple_of(layer * half, half), half)

    def unit_rows(unit, r):
        return near.at[pl.ds((unit * rows_here + r) * slots, slots), my_half, :]

    def hop(h, direction, r):
        index = 0 if direction > 0 else 1
        source = values_ref.at[r] if h == 0 else unit_rows(HOPS - direction * h, r)
        return pltpu.make_async_remote_copy(
            source, unit_rows(HOPS - direction * (h + 1), r),
            hop_send.at[h, index, r], hop_recv.at[h, index, r],
            device_id=at(direction), device_id_type=MESH)

    def across(unit, r):
        source = values_ref.at[r] if unit == HOPS else unit_rows(unit, r)
        return pltpu.make_async_remote_copy(
            source, unit_rows(unit, r), core_send.at[unit, r], core_recv.at[unit, r],
            device_id=sibling, device_id_type=MESH)

    table_copy = pltpu.make_async_copy(columns_ref, table, local_sem.at[0])
    own_copy = pltpu.make_async_copy(values_ref, own, local_sem.at[1])
    table_copy.start()
    own_copy.start()

    barrier = pltpu.get_barrier_semaphore()
    for peer in (at(1), at(-1), sibling):
        pl.semaphore_signal(barrier, inc=1, device_id=peer, device_id_type=MESH)
    pl.semaphore_wait(barrier, 3)

    for r in range(rows_here):
        for direction in (1, -1):
            hop(0, direction, r).start()
    for r in range(rows_here):
        across(HOPS, r).start()
    near[empty] = jnp.zeros((2 * half, width), near.dtype)
    near_own = [pltpu.make_async_copy(values_ref.at[r], unit_rows(HOPS, r), local_sem.at[2 + r]) for r in range(rows_here)]
    for copy in near_own:
        copy.start()
    table_copy.wait()

    @pl.loop(0, rows_here * slots)
    def _(step):
        t, k = step // slots, lax.rem(step, slots)
        i = position * rows_here + t
        j = table[k, i]
        base = lax.rem(j - position * rows_here + HOPS * rows_here + total_rows, total_rows) * slots
        there = [table[s, j] for s in range(slots)]
        for m in range(slots):
            wanted = table[m, i]
            found = empty
            for s in range(slots):
                found = jnp.where(there[s] == wanted, base + s, found)
            place[step * slots + m] = jnp.minimum(found, empty)

    for h in range(HOPS):
        for r in range(rows_here):
            for direction in (1, -1):
                hop(h, direction, r).wait_recv()
                if h + 1 < HOPS:
                    hop(h + 1, direction, r).start()
                across(HOPS - direction * (h + 1), r).start()
    own_copy.wait()
    for copy in near_own:
        copy.wait()
    for unit in range(units):
        for r in range(rows_here):
            across(unit, r).wait_recv()

    pairs = slots // 2

    @pl.loop(0, rows_here * pairs)
    def _(step):
        t, pair = step // pairs, lax.rem(step, pairs)
        left = jnp.concatenate([own[t, k] for k in range(slots)], axis=1)
        first = t * slots * slots + 2 * pair
        right = jnp.concatenate([
            jnp.concatenate([near[place[first + k * slots]], near[place[first + k * slots + 1]]], axis=1)
            for k in range(slots)], axis=0)
        product = jnp.dot(left, right, preferred_element_type=jnp.float32).astype(out_ref.dtype)
        out_ref[t, 2 * pair] = product[:, :width]
        out_ref[t, 2 * pair + 1] = product[:, width:]

    for h in range(HOPS):
        for r in range(rows_here):
            for direction in (1, -1):
                hop(h, direction, r).wait_send()
    for unit in range(units):
        for r in range(rows_here):
            across(unit, r).wait_send()


def whole_square(sizes, table, values):
    rows_here, slots, half, width = values.shape
    units = 2 * HOPS + 1
    return pl.pallas_call(
        functools.partial(whole_kernel, sizes),
        out_shape=jax.ShapeDtypeStruct(values.shape, values.dtype),
        in_specs=[pl.BlockSpec(memory_space=pl.ANY), pl.BlockSpec(memory_space=pl.ANY)],
        out_specs=pl.BlockSpec(memory_space=pltpu.VMEM),
        scratch_shapes=[
            pltpu.VMEM((units * rows_here * slots + 1, 2 * half, width), values.dtype),
            pltpu.VMEM(values.shape, values.dtype),
            pltpu.SMEM(table.shape, jnp.int32),
            pltpu.SMEM((rows_here * slots * slots,), jnp.int32),
            pltpu.SemaphoreType.DMA((HOPS, 2, rows_here)),
            pltpu.SemaphoreType.DMA((HOPS, 2, rows_here)),
            pltpu.SemaphoreType.DMA((units, rows_here)),
            pltpu.SemaphoreType.DMA((units, rows_here)),
            pltpu.SemaphoreType.DMA((2 + rows_here,)),
        ],
        compiler_params=pltpu.CompilerParams(
            collective_id=1, has_side_effects=True, vmem_limit_bytes=56 << 20),
        name="whole_square",
    )(table, values)


def shifted_mask(mask, step):
    return mask << -step if step < 0 else mask >> step


def seam_streams(col, cols_axis):
    return (col >= cols_axis - 1) | (col <= 3)


def layout(first, tail, far_first, far_tail, last_first, last_tail, behind, larger):
    lead = LAG * CHUNK

    def starts(n):
        one = larger(first + behind(tail, n), first + FIRST_LAG * CHUNK)
        two = larger(one + behind(far_first, n + 1),
                     first + behind(tail, n + 1) - behind(last_tail, n + 1) + lead)
        return one, two

    one, two = starts(0)
    one_behind, two_behind = starts(1)
    three = larger(two + behind(far_tail, 1), one_behind + lead)
    four = larger(three + behind(last_first, 2), two_behind + lead)
    return one, two, three, four, four + behind(last_tail, 2)


def stream_excess(table_ref, total_rows, rows_here, cols_axis):
    table = table_ref[...]
    slots = table.shape[0]
    lane = lax.broadcasted_iota(jnp.int32, table.shape, 1)
    place = (table - lane + REACH) & 31
    masks = jnp.sum(jnp.left_shift(jnp.ones_like(place), place), axis=0, keepdims=True)
    masks = jnp.broadcast_to(masks, (8, total_rows))
    own_row_index = lax.broadcasted_iota(jnp.int32, masks.shape, 1)
    own_row = own_row_index % rows_here

    def ahead(array, steps):
        return pltpu.roll(array, (-steps) % total_rows, 1)

    seam = seam_streams((own_row_index // rows_here) % cols_axis, cols_axis)
    most = jnp.full((1, total_rows), -STREAM, jnp.int32)
    for direction in (1, -1):
        wanted = {}
        for away in range(1, HOPS + 1):
            got = jnp.zeros_like(masks)
            for step in range(away * rows_here - rows_here + 1, away * rows_here + rows_here):
                if step > REACH:
                    continue
                step = direction * step
                there = ahead(masks, step)
                row_there = own_row + step - direction * away * rows_here
                use = (row_there >= 0) & (row_there < rows_here)
                use = use & (((there >> (REACH - step)) & 1) == 1)
                got = got | jnp.where(use, shifted_mask(there, -step), 0)
            wanted[away] = got[0:1]
        own_first = (own_row >= rows_here // 2) if direction > 0 else (own_row < rows_here // 2)

        def counts(mask):
            hits = jnp.sum((jnp.broadcast_to(mask, place.shape) >> place) & 1, axis=0, keepdims=True)
            hits = jnp.broadcast_to(hits, (8, total_rows))
            totals = []
            for part in (jnp.where(own_first, hits, 0), jnp.where(own_first, 0, hits)):
                summed = part
                for r in range(1, rows_here):
                    summed = summed + ahead(part, r)
                totals.append(summed)
            return totals

        _, tail = counts(wanted[1] | wanted[2] | wanted[3])
        far_first, far_tail = counts(wanted[2] | wanted[3])
        last_first, last_tail = counts(wanted[3])
        end = layout(rows_here // 2 * slots, tail, far_first, far_tail, last_first, last_tail,
                     lambda count, n: ahead(count, -direction * rows_here * n), jnp.maximum)[-1]
        room = jnp.where(seam, SEAM_STREAM, STREAM) if direction > 0 else STREAM
        most = jnp.maximum(most, jnp.where(own_row == 0, end - room, -STREAM)[0:1])
    return jnp.max(most)


def ones(bits):
    bits = bits - ((bits >> 1) & 0x55555555)
    bits = (bits & 0x33333333) + ((bits >> 2) & 0x33333333)
    bits = (bits + (bits >> 4)) & 0x0F0F0F0F
    return (bits * 0x01010101) >> 24


def lowest(bits, limit):
    one = bits & -bits
    index = jnp.int32(0)
    for level in range(5):
        pattern = sum(1 << b for b in range(limit) if (b >> level) & 1)
        index = index + jnp.where((one & pattern) != 0, 1 << level, 0)
    return index, bits ^ one


def sparse_kernel(sizes, columns_ref, values_ref, out_ref, excess_ref, rows_own, own, mine, every, landed, packed,
                  table, table_rows, masks, needs, order, slot_of, place,
                  unit_send, unit_recv, stream_send, stream_recv, core_send, core_recv, local_sem):
    rows_axis, cols_axis = sizes
    positions = rows_axis * cols_axis
    blocks, half, width = values_ref.shape
    rows_here, slots = out_ref.shape[:2]
    total_rows = rows_here * positions
    row, col, layer = lax.axis_index("row"), lax.axis_index("col"), lax.axis_index("layer")
    position = row * cols_axis + col
    first_row = position * rows_here
    first_rows = rows_here // 2
    first = first_rows * slots
    chunks = (STREAM - first) // CHUNK
    units = 2 * HOPS + 1
    empty = blocks + 2 * STREAM
    own_frame, other_frame = 1 - layer, layer

    def at(offset):
        there = lax.rem(position + offset + positions, positions)
        return (there // cols_axis, lax.rem(there, cols_axis), layer)

    ahead, behind = at(1 - 2 * own_frame), at(2 * own_frame - 1)
    sibling = (row, col, 1 - layer)
    halves = [pl.ds(pl.multiple_of(which * half, half), half) for which in (layer, 1 - layer)]

    def row_of(frame, r):
        return jnp.where(frame == 0, r, rows_here - 1 - r)

    def blocks_of(frame, r):
        return pl.ds(row_of(frame, r) * slots, slots)

    def stream_base(frame):
        return blocks + frame * STREAM

    def unit_copy(n, which):
        r = rows_here - 1 - n
        source = values_ref.at[blocks_of(own_frame, r)] if which == 0 else own.at[blocks_of(own_frame, r), halves[1], :]
        return pltpu.make_async_remote_copy(
            source, mine.at[pl.ds(blocks + n * slots, slots), halves[which], :],
            unit_send.at[n, which], unit_recv.at[n, which], device_id=ahead, device_id_type=MESH)

    def stream_copy(c):
        part = pl.ds(c * CHUNK, CHUNK)
        return pltpu.make_async_remote_copy(
            packed.at[part], landed.at[part], stream_send.at[c], stream_recv.at[c],
            device_id=ahead, device_id_type=MESH)

    def own_across(r):
        part = blocks_of(other_frame, r)
        return pltpu.make_async_remote_copy(
            values_ref.at[part], own.at[part, halves[0], :], core_send.at[r], core_recv.at[r],
            device_id=sibling, device_id_type=MESH)

    def unit_across():
        index = rows_here
        return pltpu.make_async_remote_copy(
            mine.at[pl.ds(blocks, first)], every.at[pl.ds(stream_base(own_frame), first)],
            core_send.at[index], core_recv.at[index], device_id=sibling, device_id_type=MESH)

    def stream_across(c):
        index = rows_here + 1 + c
        return pltpu.make_async_remote_copy(
            landed.at[pl.ds(c * CHUNK, CHUNK)], every.at[pl.ds(stream_base(own_frame) + first + c * CHUNK, CHUNK)],
            core_send.at[index], core_recv.at[index], device_id=sibling, device_id_type=MESH)

    table_copy = pltpu.make_async_copy(columns_ref, table, local_sem.at[0])
    lanes_copy = pltpu.make_async_copy(columns_ref, table_rows, local_sem.at[1])
    rows_copy = pltpu.make_async_copy(values_ref, rows_own, local_sem.at[2])
    own_copy = pltpu.make_async_copy(values_ref, own.at[:, halves[0], :], local_sem.at[3])
    for copy in (table_copy, own_copy, lanes_copy, rows_copy):
        copy.start()

    barrier = pltpu.get_barrier_semaphore()
    for peer in (behind, sibling):
        pl.semaphore_signal(barrier, inc=1, device_id=peer, device_id_type=MESH)
    pl.semaphore_wait(barrier, 2)

    for n in range(first_rows):
        unit_copy(n, 0).start()
        own_across(rows_here - 1 - n).start()
    for r in reversed(range(rows_here - first_rows)):
        own_across(r).start()
    every[empty] = jnp.zeros((2 * half, width), every.dtype)

    table_copy.wait()
    zero = jnp.int32(0)

    def wrapped(value):
        value = jnp.where(value < 0, value + total_rows, value)
        return jnp.where(value >= total_rows, value - total_rows, value)

    def row_at(frame, r):
        return wrapped(first_row + row_of(frame, r))

    def distance(frame, entry, i):
        return (jnp.where(frame == 0, entry - i, i - entry) + REACH) & 31

    def fill_masks(frame):
        @pl.loop(0, units * rows_here)
        def _(n):
            i = row_at(frame, n - HOPS * rows_here)
            mask = zero
            for k in range(slots):
                mask = mask | (jnp.int32(1) << distance(frame, table[k, i], i))
            masks[n] = mask

    def unit_mask(unit, r):
        return masks[rows_here * (unit + HOPS) + r]

    def need(source, receiver, r):
        got = zero
        for t in range(rows_here):
            step = rows_here * (source - receiver) + r - t
            if abs(step) <= REACH:
                mask = unit_mask(receiver, t)
                got = got | jnp.where(((mask >> (step + REACH)) & 1) == 1, shifted_mask(mask, step), 0)
        return got

    def needs_at(back, n, which):
        return (back * rows_here + n) * 3 + which

    def fill_needs(back):
        for n in range(rows_here):
            near, far, last = (need(-back, away - back, rows_here - 1 - n) for away in (1, 2, 3))
            for which, bits in enumerate((near | far | last, far | last, last)):
                needs[needs_at(back, n, which)] = bits

    def of_row(frame, back, n):
        r = rows_here - 1 - n
        j = row_at(frame, r - back * rows_here)
        start = row_of(frame, r) * slots
        wanted = [needs[needs_at(back, n, which)] for which in range(3)]
        found = []
        for s in range(slots):
            e = distance(frame, table[s, j], j)
            found.append((start + s, *((bits >> e) & 1 for bits in wanted)))
        return found

    def count(back, which, rows):
        total = zero
        for n in rows:
            total = total + ones(needs[needs_at(back, n, which)] & unit_mask(-back, rows_here - 1 - n))
        return total

    firsts, tails = range(first_rows), range(first_rows, rows_here)

    def natural(n, s):
        return row_of(own_frame, rows_here - 1 - n) * slots + s

    fill_masks(own_frame)
    fill_needs(0)
    bits = zero
    for n in tails:
        for s, (_, near, _, _) in enumerate(of_row(own_frame, 0, n)):
            bits = bits | (near << ((n - first_rows) * slots + s))

    def arrange_own(s, bits):
        found, bits = lowest(bits, blocks - first)
        order[s] = natural(first_rows + found // slots, lax.rem(found, slots))
        return bits

    lax.fori_loop(first, blocks, arrange_own, bits)

    own_copy.wait()
    for r in reversed(range(rows_here)):
        own_across(r).wait_recv()
        n = rows_here - 1 - r
        if n < first_rows:
            unit_copy(n, 1).start()
    mine_copy = pltpu.make_async_copy(own, mine.at[pl.ds(0, blocks)], local_sem.at[4])
    every_copy = pltpu.make_async_copy(own, every.at[pl.ds(0, blocks)], local_sem.at[5])
    mine_copy.start()
    every_copy.start()

    right = own_frame == 0
    sends_short = right & seam_streams(col, cols_axis)
    seam_here = seam_streams(lax.rem(col + cols_axis - 1, cols_axis), cols_axis)
    gets_short = right & seam_here
    other_short = jnp.logical_not(right) & seam_here

    def unless(short, c, step):
        if first + c * CHUNK >= SEAM_STREAM:
            pl.when(jnp.logical_not(short))(step)
        else:
            step()

    def pack(c, source):
        def step():
            for s in range(c * CHUNK, (c + 1) * CHUNK):
                packed[s] = source[order[first + s]]
            stream_copy(c).start()
        unless(sends_short, c, step)

    for c in range(FIRST_LAG):
        pack(c, own)

    def fill_slots(frame, with_order):
        for back in range(1, HOPS + 1):
            fill_needs(back)
        tail = [count(back, 0, tails) for back in range(HOPS + 1)]
        far_first, far_tail = ([count(back, 1, rows) for back in range(HOPS + 1)] for rows in (firsts, tails))
        last_first, last_tail = ([count(back, 2, rows) for back in range(HOPS + 1)] for rows in (firsts, tails))

        def starts(here):
            return layout(first, tail, far_first, far_tail, last_first, last_tail,
                          lambda counts, n: counts[min(here + n, HOPS)], jnp.maximum)

        one_in, two_in, three_in, four_in, _ = starts(1)
        base = stream_base(frame)

        def unit_at(back):
            return jnp.where(frame == 0, HOPS - back, HOPS + back) * blocks

        def note(back, block, spot):
            slot_of[unit_at(back) + block] = base + jnp.clip(spot, 0, STREAM - 1)

        words = []
        seen = zero
        for rows in (firsts, tails):
            last_bits = far_bits = zero
            for n in rows:
                for s, (block, near, far, last) in enumerate(of_row(frame, 1, n)):
                    step = (n - rows[0]) * slots + s
                    if with_order:
                        last_bits = last_bits | (last << step)
                        far_bits = far_bits | ((far & (1 - last)) << step)
                    if rows is firsts:
                        note(1, block, step)
                    else:
                        note(1, block, first + seen)
                        seen = seen + near
            words += [last_bits, far_bits]

        for rows, start, total, later in ((firsts, one_in, last_first[2], three_in), (tails, two_in, last_tail[2], four_in)):
            last_spot, far_spot, spot = start, start + total, later
            for n in rows:
                for block, _, far, last in of_row(frame, 2, n):
                    note(2, block, jnp.where(last == 1, last_spot, far_spot))
                    last_spot = last_spot + last
                    far_spot = far_spot + (far & (1 - last))
                for block, _, _, last in of_row(frame, 3, n):
                    note(3, block, spot)
                    spot = spot + last
        if not with_order:
            return

        one, two, three, four, _ = starts(0)
        unit_behind = unit_at(1)

        def arrange(with_own, s, carry):
            bits_one, bits_two, bits_three, bits_four = carry
            from_first = s < two
            use_last = jnp.where(from_first, bits_one, bits_three) != 0
            bits = jnp.where(from_first, jnp.where(use_last, bits_one, bits_two),
                             jnp.where(use_last, bits_three, bits_four))
            found, rest = lowest(bits, first)
            n = jnp.where(from_first, 0, first_rows) + found // slots
            spot = slot_of[unit_behind + natural(n, lax.rem(found, slots))] - base
            spot = jnp.where(s >= three, one_in + s - three, spot)
            spot = jnp.where(s >= four, two_in + s - four, spot)
            spot = blocks + jnp.clip(spot, 0, STREAM - 1)
            active = True
            if with_own:
                active = s >= one
                spot = jnp.where(active, spot, order[s])
            order[s] = spot
            pick = [from_first & use_last, from_first & ~use_last, ~from_first & use_last, ~from_first & ~use_last]
            return tuple(jnp.where(p & active, rest, b) for p, b in zip(pick, carry))

        carry = lax.fori_loop(first + FIRST_LAG * CHUNK, blocks, functools.partial(arrange, True), tuple(words))
        lax.fori_loop(blocks, STREAM, functools.partial(arrange, False), carry)

    fill_slots(own_frame, True)
    fill_masks(other_frame)
    fill_slots(other_frame, False)

    @pl.loop(0, blocks)
    def _(step):
        slot_of[HOPS * blocks + step] = step

    def find(step):
        t, k = step // slots, lax.rem(step, slots)
        i = first_row + t
        j = table[k, i]
        base = jnp.minimum(wrapped(j - first_row + HOPS * rows_here), units * rows_here - 1) * slots
        there = [table[s, j] for s in range(slots)]
        for m in range(slots):
            wanted = table[m, i]
            found = jnp.int32(-1)
            for s in range(slots):
                found = jnp.where(there[s] == wanted, s, found)
            spot = slot_of[base + jnp.maximum(found, 0)]
            place[step * slots + m] = jnp.where(found < 0, empty, spot)

    def take(c):
        def step():
            stream_copy(c).wait_recv()
            stream_across(c).start()
            got = landed[pl.ds(c * CHUNK, CHUNK)]
            mine[pl.ds(blocks + first + c * CHUNK, CHUNK)] = got
            every[pl.ds(stream_base(own_frame) + first + c * CHUNK, CHUNK)] = got
        unless(gets_short, c, step)

    mine_copy.wait()
    for n in range(first_rows):
        for which in range(2):
            unit_copy(n, which).wait_recv()
    unit_across().start()
    unit_every = pltpu.make_async_copy(
        mine.at[pl.ds(blocks, first)], every.at[pl.ds(stream_base(own_frame), first)], local_sem.at[6])
    unit_every.start()

    shares = blocks // CHUNK
    for c in range(FIRST_LAG, chunks):
        if c >= LAG:
            take(c - LAG)
        pack(c, mine)
        n = c - FIRST_LAG
        if n < shares:
            pl.loop(n * blocks // shares, (n + 1) * blocks // shares)(find)
    lanes_copy.wait()
    excess_ref[0, 0] = stream_excess(table_rows, total_rows, rows_here, cols_axis)
    def wait_sends(start, end):
        for c in range(start, end):
            unless(sends_short, c, lambda c=c: stream_copy(c).wait_send())
            unless(gets_short, c, lambda c=c: stream_across(c).wait_send())

    early_chunks = (SEAM_STREAM - first) // CHUNK - 2 * LAG
    for r in range(rows_here):
        own_across(r).wait_send()
    for n in range(first_rows):
        for which in range(2):
            unit_copy(n, which).wait_send()
    unit_across().wait_send()
    wait_sends(0, early_chunks)

    for c in range(chunks - LAG, chunks):
        take(c)

    rows_copy.wait()
    every_copy.wait()
    unit_every.wait()
    unit_across().wait_recv()
    for c in range(chunks):
        unless(other_short, c, lambda c=c: stream_across(c).wait_recv())

    pairs = slots // 2

    @pl.loop(0, rows_here * pairs, unroll=20)
    def _(step):
        t, pair = step // pairs, lax.rem(step, pairs)
        start = t * slots * slots + 2 * pair
        left = jnp.concatenate([rows_own[t * slots + k] for k in range(slots)], axis=1)
        rhs = jnp.concatenate([
            jnp.concatenate([every[place[start + k * slots]], every[place[start + k * slots + 1]]], axis=1)
            for k in range(slots)], axis=0)
        product = jnp.dot(left, rhs, preferred_element_type=jnp.float32).astype(out_ref.dtype)
        out_ref[t, 2 * pair] = product[:, :width]
        out_ref[t, 2 * pair + 1] = product[:, width:]

    wait_sends(early_chunks, chunks)


def sparse_square(sizes, table, values):
    rows_here, slots, half, width = values.shape
    blocks = rows_here * slots
    first_rows = rows_here // 2
    units = 2 * HOPS + 1
    chunks = (STREAM - first_rows * slots) // CHUNK
    crossings = rows_here + 1 + chunks

    def whole_blocks(count):
        return pltpu.VMEM((count, 2 * half, width), values.dtype)

    return pl.pallas_call(
        functools.partial(sparse_kernel, sizes),
        out_shape=[jax.ShapeDtypeStruct(values.shape, values.dtype), jax.ShapeDtypeStruct((1, 1), jnp.int32)],
        in_specs=[pl.BlockSpec(memory_space=pl.ANY), pl.BlockSpec(memory_space=pl.ANY)],
        out_specs=[pl.BlockSpec(memory_space=pltpu.VMEM), pl.BlockSpec(memory_space=pltpu.SMEM)],
        scratch_shapes=[
            pltpu.VMEM((blocks, half, width), values.dtype),
            whole_blocks(blocks),
            whole_blocks(blocks + STREAM),
            whole_blocks(blocks + 2 * STREAM + 1),
            whole_blocks(chunks * CHUNK),
            whole_blocks(chunks * CHUNK),
            pltpu.SMEM(table.shape, jnp.int32),
            pltpu.VMEM(table.shape, jnp.int32),
            pltpu.SMEM((units * rows_here,), jnp.int32),
            pltpu.SMEM(((HOPS + 1) * rows_here * 3,), jnp.int32),
            pltpu.SMEM((STREAM,), jnp.int32),
            pltpu.SMEM((units * blocks,), jnp.int32),
            pltpu.SMEM((blocks * slots,), jnp.int32),
            pltpu.SemaphoreType.DMA((first_rows, 2)),
            pltpu.SemaphoreType.DMA((first_rows, 2)),
            pltpu.SemaphoreType.DMA((chunks,)),
            pltpu.SemaphoreType.DMA((chunks,)),
            pltpu.SemaphoreType.DMA((crossings,)),
            pltpu.SemaphoreType.DMA((crossings,)),
            pltpu.SemaphoreType.DMA((7,)),
        ],
        compiler_params=pltpu.CompilerParams(
            collective_id=0, has_side_effects=True, vmem_limit_bytes=56 << 20),
        name="sparse_square",
    )(table, values.reshape(blocks, half, width))


def on_device(sizes, values, columns):
    table = columns.T
    square, excess = sparse_square(sizes, table, values)
    return lax.cond(excess[0, 0] > 0,
                    lambda: whole_square(sizes, table, values),
                    lambda: square)


def solution(mesh):
    return jax.shard_map(
        functools.partial(on_device, (mesh.shape["row"], mesh.shape["col"])),
        mesh=mesh,
        in_specs=(P(("row", "col"), None, "layer", None), P()),
        out_specs=P(("row", "col"), None, "layer", None),
        check_vma=False,
    )
```

```python
import functools

import jax
import jax.numpy as jnp
from jax import lax
from jax.experimental import pallas as pl
from jax.experimental.pallas import tpu as pltpu
from jax.sharding import PartitionSpec as P

HOPS = 3
REACH = 12
SPAN = 2 * REACH
STREAM = 92
SEAM_STREAM = 80
CHUNK = 4
LAG = 4
FIRST_LAG = 3
MESH = pl.DeviceIdType.MESH


def whole_kernel(sizes, columns_ref, values_ref, out_ref, near, own, table, place,
                 hop_send, hop_recv, core_send, core_recv, local_sem):
    rows_axis, cols_axis = sizes
    positions = rows_axis * cols_axis
    rows_here, slots, half, width = values_ref.shape
    total_rows = rows_here * positions
    row, col, layer = lax.axis_index("row"), lax.axis_index("col"), lax.axis_index("layer")
    position = row * cols_axis + col
    units = 2 * HOPS + 1
    empty = units * rows_here * slots

    def at(offset):
        there = lax.rem(position + offset + positions, positions)
        return (there // cols_axis, lax.rem(there, cols_axis), layer)

    sibling = (row, col, 1 - layer)
    my_half = pl.ds(pl.multiple_of(layer * half, half), half)

    def unit_rows(unit, r):
        return near.at[pl.ds((unit * rows_here + r) * slots, slots), my_half, :]

    def hop(h, direction, r):
        index = 0 if direction > 0 else 1
        source = values_ref.at[r] if h == 0 else unit_rows(HOPS - direction * h, r)
        return pltpu.make_async_remote_copy(
            source, unit_rows(HOPS - direction * (h + 1), r),
            hop_send.at[h, index, r], hop_recv.at[h, index, r],
            device_id=at(direction), device_id_type=MESH)

    def across(unit, r):
        source = values_ref.at[r] if unit == HOPS else unit_rows(unit, r)
        return pltpu.make_async_remote_copy(
            source, unit_rows(unit, r), core_send.at[unit, r], core_recv.at[unit, r],
            device_id=sibling, device_id_type=MESH)

    table_copy = pltpu.make_async_copy(columns_ref, table, local_sem.at[0])
    own_copy = pltpu.make_async_copy(values_ref, own, local_sem.at[1])
    table_copy.start()
    own_copy.start()

    barrier = pltpu.get_barrier_semaphore()
    for peer in (at(1), at(-1), sibling):
        pl.semaphore_signal(barrier, inc=1, device_id=peer, device_id_type=MESH)
    pl.semaphore_wait(barrier, 3)

    for r in range(rows_here):
        for direction in (1, -1):
            hop(0, direction, r).start()
    for r in range(rows_here):
        across(HOPS, r).start()
    near[empty] = jnp.zeros((2 * half, width), near.dtype)
    near_own = [pltpu.make_async_copy(values_ref.at[r], unit_rows(HOPS, r), local_sem.at[2 + r]) for r in range(rows_here)]
    for copy in near_own:
        copy.start()
    table_copy.wait()

    @pl.loop(0, rows_here * slots)
    def _(step):
        t, k = step // slots, lax.rem(step, slots)
        i = position * rows_here + t
        j = table[k, i]
        base = lax.rem(j - position * rows_here + HOPS * rows_here + total_rows, total_rows) * slots
        there = [table[s, j] for s in range(slots)]
        for m in range(slots):
            wanted = table[m, i]
            found = empty
            for s in range(slots):
                found = jnp.where(there[s] == wanted, base + s, found)
            place[step * slots + m] = jnp.minimum(found, empty)

    for h in range(HOPS):
        for r in range(rows_here):
            for direction in (1, -1):
                hop(h, direction, r).wait_recv()
                if h + 1 < HOPS:
                    hop(h + 1, direction, r).start()
                across(HOPS - direction * (h + 1), r).start()
    own_copy.wait()
    for copy in near_own:
        copy.wait()
    for unit in range(units):
        for r in range(rows_here):
            across(unit, r).wait_recv()

    pairs = slots // 2

    @pl.loop(0, rows_here * pairs)
    def _(step):
        t, pair = step // pairs, lax.rem(step, pairs)
        left = jnp.concatenate([own[t, k] for k in range(slots)], axis=1)
        first = t * slots * slots + 2 * pair
        right = jnp.concatenate([
            jnp.concatenate([near[place[first + k * slots]], near[place[first + k * slots + 1]]], axis=1)
            for k in range(slots)], axis=0)
        product = jnp.dot(left, right, preferred_element_type=jnp.float32).astype(out_ref.dtype)
        out_ref[t, 2 * pair] = product[:, :width]
        out_ref[t, 2 * pair + 1] = product[:, width:]

    for h in range(HOPS):
        for r in range(rows_here):
            for direction in (1, -1):
                hop(h, direction, r).wait_send()
    for unit in range(units):
        for r in range(rows_here):
            across(unit, r).wait_send()


def whole_square(sizes, table, values):
    rows_here, slots, half, width = values.shape
    units = 2 * HOPS + 1
    return pl.pallas_call(
        functools.partial(whole_kernel, sizes),
        out_shape=jax.ShapeDtypeStruct(values.shape, values.dtype),
        in_specs=[pl.BlockSpec(memory_space=pl.ANY), pl.BlockSpec(memory_space=pl.ANY)],
        out_specs=pl.BlockSpec(memory_space=pltpu.VMEM),
        scratch_shapes=[
            pltpu.VMEM((units * rows_here * slots + 1, 2 * half, width), values.dtype),
            pltpu.VMEM(values.shape, values.dtype),
            pltpu.SMEM(table.shape, jnp.int32),
            pltpu.SMEM((rows_here * slots * slots,), jnp.int32),
            pltpu.SemaphoreType.DMA((HOPS, 2, rows_here)),
            pltpu.SemaphoreType.DMA((HOPS, 2, rows_here)),
            pltpu.SemaphoreType.DMA((units, rows_here)),
            pltpu.SemaphoreType.DMA((units, rows_here)),
            pltpu.SemaphoreType.DMA((2 + rows_here,)),
        ],
        compiler_params=pltpu.CompilerParams(
            collective_id=1, has_side_effects=True, vmem_limit_bytes=56 << 20),
        name="whole_square",
    )(table, values)


def shifted_mask(mask, step):
    return mask << -step if step < 0 else mask >> step


def seam_streams(col, cols_axis):
    return (col >= cols_axis - 1) | (col <= 3)


def layout(first, tail, far_first, far_tail, last_first, last_tail, behind, larger):
    lead = LAG * CHUNK

    def starts(n):
        one = larger(first + behind(tail, n), first + FIRST_LAG * CHUNK)
        two = larger(one + behind(far_first, n + 1),
                     first + behind(tail, n + 1) - behind(last_tail, n + 1) + lead)
        return one, two

    one, two = starts(0)
    one_behind, two_behind = starts(1)
    three = larger(two + behind(far_tail, 1), one_behind + lead)
    four = larger(three + behind(last_first, 2), two_behind + lead)
    return one, two, three, four, four + behind(last_tail, 2)


def stream_excess(table_ref, total_rows, rows_here, cols_axis):
    table = table_ref[...]
    slots = table.shape[0]
    lane = lax.broadcasted_iota(jnp.int32, table.shape, 1)
    place = (table - lane + REACH) & 31
    masks = jnp.sum(jnp.left_shift(jnp.ones_like(place), place), axis=0, keepdims=True)
    masks = jnp.broadcast_to(masks, (8, total_rows))
    own_row_index = lax.broadcasted_iota(jnp.int32, masks.shape, 1)
    own_row = own_row_index % rows_here

    def ahead(array, steps):
        return pltpu.roll(array, (-steps) % total_rows, 1)

    seam = seam_streams((own_row_index // rows_here) % cols_axis, cols_axis)
    most = jnp.full((1, total_rows), -STREAM, jnp.int32)
    for direction in (1, -1):
        wanted = {}
        for away in range(1, HOPS + 1):
            got = jnp.zeros_like(masks)
            for step in range(away * rows_here - rows_here + 1, away * rows_here + rows_here):
                if step > REACH:
                    continue
                step = direction * step
                there = ahead(masks, step)
                row_there = own_row + step - direction * away * rows_here
                use = (row_there >= 0) & (row_there < rows_here)
                use = use & (((there >> (REACH - step)) & 1) == 1)
                got = got | jnp.where(use, shifted_mask(there, -step), 0)
            wanted[away] = got[0:1]
        own_first = (own_row >= rows_here // 2) if direction > 0 else (own_row < rows_here // 2)

        def counts(mask):
            hits = jnp.sum((jnp.broadcast_to(mask, place.shape) >> place) & 1, axis=0, keepdims=True)
            hits = jnp.broadcast_to(hits, (8, total_rows))
            totals = []
            for part in (jnp.where(own_first, hits, 0), jnp.where(own_first, 0, hits)):
                summed = part
                for r in range(1, rows_here):
                    summed = summed + ahead(part, r)
                totals.append(summed)
            return totals

        _, tail = counts(wanted[1] | wanted[2] | wanted[3])
        far_first, far_tail = counts(wanted[2] | wanted[3])
        last_first, last_tail = counts(wanted[3])
        end = layout(rows_here // 2 * slots, tail, far_first, far_tail, last_first, last_tail,
                     lambda count, n: ahead(count, -direction * rows_here * n), jnp.maximum)[-1]
        room = jnp.where(seam, SEAM_STREAM, STREAM) if direction > 0 else STREAM
        most = jnp.maximum(most, jnp.where(own_row == 0, end - room, -STREAM)[0:1])
    return jnp.max(most)


def ones(bits):
    bits = bits - ((bits >> 1) & 0x55555555)
    bits = (bits & 0x33333333) + ((bits >> 2) & 0x33333333)
    bits = (bits + (bits >> 4)) & 0x0F0F0F0F
    return (bits * 0x01010101) >> 24


def lowest(bits, limit):
    one = bits & -bits
    index = jnp.int32(0)
    for level in range(5):
        pattern = sum(1 << b for b in range(limit) if (b >> level) & 1)
        index = index + jnp.where((one & pattern) != 0, 1 << level, 0)
    return index, bits ^ one


def sparse_kernel(sizes, columns_ref, values_ref, out_ref, excess_ref, rows_own, own, mine, every, landed, packed,
                  table, table_rows, masks, needs, order, slot_of, place,
                  unit_send, unit_recv, stream_send, stream_recv, core_send, core_recv, local_sem):
    rows_axis, cols_axis = sizes
    positions = rows_axis * cols_axis
    blocks, half, width = values_ref.shape
    rows_here, slots = out_ref.shape[:2]
    total_rows = rows_here * positions
    row, col, layer = lax.axis_index("row"), lax.axis_index("col"), lax.axis_index("layer")
    position = row * cols_axis + col
    first_row = position * rows_here
    first_rows = rows_here // 2
    first = first_rows * slots
    chunks = (STREAM - first) // CHUNK
    units = 2 * HOPS + 1
    empty = blocks + 2 * STREAM
    own_frame, other_frame = 1 - layer, layer

    def at(offset):
        there = lax.rem(position + offset + positions, positions)
        return (there // cols_axis, lax.rem(there, cols_axis), layer)

    ahead, behind = at(1 - 2 * own_frame), at(2 * own_frame - 1)
    sibling = (row, col, 1 - layer)
    halves = [pl.ds(pl.multiple_of(which * half, half), half) for which in (layer, 1 - layer)]

    def row_of(frame, r):
        return jnp.where(frame == 0, r, rows_here - 1 - r)

    def blocks_of(frame, r):
        return pl.ds(row_of(frame, r) * slots, slots)

    def stream_base(frame):
        return blocks + frame * STREAM

    def unit_copy(n, which):
        r = rows_here - 1 - n
        source = values_ref.at[blocks_of(own_frame, r)] if which == 0 else own.at[blocks_of(own_frame, r), halves[1], :]
        return pltpu.make_async_remote_copy(
            source, mine.at[pl.ds(blocks + n * slots, slots), halves[which], :],
            unit_send.at[n, which], unit_recv.at[n, which], device_id=ahead, device_id_type=MESH)

    def stream_copy(c):
        part = pl.ds(c * CHUNK, CHUNK)
        return pltpu.make_async_remote_copy(
            packed.at[part], landed.at[part], stream_send.at[c], stream_recv.at[c],
            device_id=ahead, device_id_type=MESH)

    def own_across(r):
        part = blocks_of(other_frame, r)
        return pltpu.make_async_remote_copy(
            values_ref.at[part], own.at[part, halves[0], :], core_send.at[r], core_recv.at[r],
            device_id=sibling, device_id_type=MESH)

    def unit_across():
        index = rows_here
        return pltpu.make_async_remote_copy(
            mine.at[pl.ds(blocks, first)], every.at[pl.ds(stream_base(own_frame), first)],
            core_send.at[index], core_recv.at[index], device_id=sibling, device_id_type=MESH)

    def stream_across(c):
        index = rows_here + 1 + c
        return pltpu.make_async_remote_copy(
            landed.at[pl.ds(c * CHUNK, CHUNK)], every.at[pl.ds(stream_base(own_frame) + first + c * CHUNK, CHUNK)],
            core_send.at[index], core_recv.at[index], device_id=sibling, device_id_type=MESH)

    table_copy = pltpu.make_async_copy(columns_ref, table, local_sem.at[0])
    lanes_copy = pltpu.make_async_copy(columns_ref, table_rows, local_sem.at[1])
    rows_copy = pltpu.make_async_copy(values_ref, rows_own, local_sem.at[2])
    own_copy = pltpu.make_async_copy(values_ref, own.at[:, halves[0], :], local_sem.at[3])
    for copy in (table_copy, own_copy, lanes_copy, rows_copy):
        copy.start()

    barrier = pltpu.get_barrier_semaphore()
    for peer in (behind, sibling):
        pl.semaphore_signal(barrier, inc=1, device_id=peer, device_id_type=MESH)
    pl.semaphore_wait(barrier, 2)

    for n in range(first_rows):
        unit_copy(n, 0).start()
        own_across(rows_here - 1 - n).start()
    for r in reversed(range(rows_here - first_rows)):
        own_across(r).start()
    every[empty] = jnp.zeros((2 * half, width), every.dtype)

    table_copy.wait()
    zero = jnp.int32(0)

    def wrapped(value):
        value = jnp.where(value < 0, value + total_rows, value)
        return jnp.where(value >= total_rows, value - total_rows, value)

    def row_at(frame, r):
        return wrapped(first_row + row_of(frame, r))

    def distance(frame, entry, i):
        return (jnp.where(frame == 0, entry - i, i - entry) + REACH) & 31

    def fill_masks(frame):
        @pl.loop(0, units * rows_here)
        def _(n):
            i = row_at(frame, n - HOPS * rows_here)
            mask = zero
            for k in range(slots):
                mask = mask | (jnp.int32(1) << distance(frame, table[k, i], i))
            masks[n] = mask

    def unit_mask(unit, r):
        return masks[rows_here * (unit + HOPS) + r]

    def need(source, receiver, r):
        got = zero
        for t in range(rows_here):
            step = rows_here * (source - receiver) + r - t
            if abs(step) <= REACH:
                mask = unit_mask(receiver, t)
                got = got | jnp.where(((mask >> (step + REACH)) & 1) == 1, shifted_mask(mask, step), 0)
        return got

    def needs_at(back, n, which):
        return (back * rows_here + n) * 3 + which

    def fill_needs(back):
        for n in range(rows_here):
            near, far, last = (need(-back, away - back, rows_here - 1 - n) for away in (1, 2, 3))
            for which, bits in enumerate((near | far | last, far | last, last)):
                needs[needs_at(back, n, which)] = bits

    def of_row(frame, back, n):
        r = rows_here - 1 - n
        j = row_at(frame, r - back * rows_here)
        start = row_of(frame, r) * slots
        wanted = [needs[needs_at(back, n, which)] for which in range(3)]
        found = []
        for s in range(slots):
            e = distance(frame, table[s, j], j)
            found.append((start + s, *((bits >> e) & 1 for bits in wanted)))
        return found

    def count(back, which, rows):
        total = zero
        for n in rows:
            total = total + ones(needs[needs_at(back, n, which)] & unit_mask(-back, rows_here - 1 - n))
        return total

    firsts, tails = range(first_rows), range(first_rows, rows_here)

    def natural(n, s):
        return row_of(own_frame, rows_here - 1 - n) * slots + s

    fill_masks(own_frame)
    fill_needs(0)
    bits = zero
    for n in tails:
        for s, (_, near, _, _) in enumerate(of_row(own_frame, 0, n)):
            bits = bits | (near << ((n - first_rows) * slots + s))

    def arrange_own(s, bits):
        found, bits = lowest(bits, blocks - first)
        order[s] = natural(first_rows + found // slots, lax.rem(found, slots))
        return bits

    lax.fori_loop(first, blocks, arrange_own, bits)

    own_copy.wait()
    for r in reversed(range(rows_here)):
        own_across(r).wait_recv()
        n = rows_here - 1 - r
        if n < first_rows:
            unit_copy(n, 1).start()
    mine_copy = pltpu.make_async_copy(own, mine.at[pl.ds(0, blocks)], local_sem.at[4])
    every_copy = pltpu.make_async_copy(own, every.at[pl.ds(0, blocks)], local_sem.at[5])
    mine_copy.start()
    every_copy.start()

    right = own_frame == 0
    sends_short = right & seam_streams(col, cols_axis)
    seam_here = seam_streams(lax.rem(col + cols_axis - 1, cols_axis), cols_axis)
    gets_short = right & seam_here
    other_short = jnp.logical_not(right) & seam_here

    def unless(short, c, step):
        if first + c * CHUNK >= SEAM_STREAM:
            pl.when(jnp.logical_not(short))(step)
        else:
            step()

    def pack(c, source):
        def step():
            for s in range(c * CHUNK, (c + 1) * CHUNK):
                packed[s] = source[order[first + s]]
            stream_copy(c).start()
        unless(sends_short, c, step)

    for c in range(FIRST_LAG):
        pack(c, own)

    def fill_slots(frame, with_order):
        for back in range(1, HOPS + 1):
            fill_needs(back)
        tail = [count(back, 0, tails) for back in range(HOPS + 1)]
        far_first, far_tail = ([count(back, 1, rows) for back in range(HOPS + 1)] for rows in (firsts, tails))
        last_first, last_tail = ([count(back, 2, rows) for back in range(HOPS + 1)] for rows in (firsts, tails))

        def starts(here):
            return layout(first, tail, far_first, far_tail, last_first, last_tail,
                          lambda counts, n: counts[min(here + n, HOPS)], jnp.maximum)

        one_in, two_in, three_in, four_in, _ = starts(1)
        base = stream_base(frame)

        def unit_at(back):
            return jnp.where(frame == 0, HOPS - back, HOPS + back) * blocks

        def note(back, block, spot):
            slot_of[unit_at(back) + block] = base + jnp.clip(spot, 0, STREAM - 1)

        words = []
        seen = zero
        for rows in (firsts, tails):
            last_bits = far_bits = zero
            for n in rows:
                for s, (block, near, far, last) in enumerate(of_row(frame, 1, n)):
                    step = (n - rows[0]) * slots + s
                    if with_order:
                        last_bits = last_bits | (last << step)
                        far_bits = far_bits | ((far & (1 - last)) << step)
                    if rows is firsts:
                        note(1, block, step)
                    else:
                        note(1, block, first + seen)
                        seen = seen + near
            words += [last_bits, far_bits]

        for rows, start, total, later in ((firsts, one_in, last_first[2], three_in), (tails, two_in, last_tail[2], four_in)):
            last_spot, far_spot, spot = start, start + total, later
            for n in rows:
                for block, _, far, last in of_row(frame, 2, n):
                    note(2, block, jnp.where(last == 1, last_spot, far_spot))
                    last_spot = last_spot + last
                    far_spot = far_spot + (far & (1 - last))
                for block, _, _, last in of_row(frame, 3, n):
                    note(3, block, spot)
                    spot = spot + last
        if not with_order:
            return

        one, two, three, four, _ = starts(0)
        unit_behind = unit_at(1)

        def arrange(with_own, s, carry):
            bits_one, bits_two, bits_three, bits_four = carry
            from_first = s < two
            use_last = jnp.where(from_first, bits_one, bits_three) != 0
            bits = jnp.where(from_first, jnp.where(use_last, bits_one, bits_two),
                             jnp.where(use_last, bits_three, bits_four))
            found, rest = lowest(bits, first)
            n = jnp.where(from_first, 0, first_rows) + found // slots
            spot = slot_of[unit_behind + natural(n, lax.rem(found, slots))] - base
            spot = jnp.where(s >= three, one_in + s - three, spot)
            spot = jnp.where(s >= four, two_in + s - four, spot)
            spot = blocks + jnp.clip(spot, 0, STREAM - 1)
            active = True
            if with_own:
                active = s >= one
                spot = jnp.where(active, spot, order[s])
            order[s] = spot
            pick = [from_first & use_last, from_first & ~use_last, ~from_first & use_last, ~from_first & ~use_last]
            return tuple(jnp.where(p & active, rest, b) for p, b in zip(pick, carry))

        carry = lax.fori_loop(first + FIRST_LAG * CHUNK, blocks, functools.partial(arrange, True), tuple(words))
        lax.fori_loop(blocks, STREAM, functools.partial(arrange, False), carry)

    fill_slots(own_frame, True)
    fill_masks(other_frame)
    fill_slots(other_frame, False)

    @pl.loop(0, blocks)
    def _(step):
        slot_of[HOPS * blocks + step] = step

    def find(step):
        t, k = step // slots, lax.rem(step, slots)
        i = first_row + t
        j = table[k, i]
        base = jnp.minimum(wrapped(j - first_row + HOPS * rows_here), units * rows_here - 1) * slots
        there = [table[s, j] for s in range(slots)]
        for m in range(slots):
            wanted = table[m, i]
            found = jnp.int32(-1)
            for s in range(slots):
                found = jnp.where(there[s] == wanted, s, found)
            spot = slot_of[base + jnp.maximum(found, 0)]
            place[step * slots + m] = jnp.where(found < 0, empty, spot)

    def take(c):
        def step():
            stream_copy(c).wait_recv()
            stream_across(c).start()
            got = landed[pl.ds(c * CHUNK, CHUNK)]
            if c < chunks - LAG:
                mine[pl.ds(blocks + first + c * CHUNK, CHUNK)] = got
            every[pl.ds(stream_base(own_frame) + first + c * CHUNK, CHUNK)] = got
        unless(gets_short, c, step)

    mine_copy.wait()
    for n in range(first_rows):
        for which in range(2):
            unit_copy(n, which).wait_recv()
    unit_across().start()
    unit_every = pltpu.make_async_copy(
        mine.at[pl.ds(blocks, first)], every.at[pl.ds(stream_base(own_frame), first)], local_sem.at[6])
    unit_every.start()

    shares = blocks // CHUNK
    for c in range(FIRST_LAG, chunks):
        if c >= LAG:
            take(c - LAG)
        pack(c, mine)
        n = c - FIRST_LAG
        if n < shares:
            pl.loop(n * blocks // shares, (n + 1) * blocks // shares)(find)
    lanes_copy.wait()
    excess_ref[0, 0] = stream_excess(table_rows, total_rows, rows_here, cols_axis)
    def wait_sends(start, end):
        for c in range(start, end):
            unless(sends_short, c, lambda c=c: stream_copy(c).wait_send())
            unless(gets_short, c, lambda c=c: stream_across(c).wait_send())

    early_chunks = (SEAM_STREAM - first) // CHUNK - 2 * LAG
    for r in range(rows_here):
        own_across(r).wait_send()
    for n in range(first_rows):
        for which in range(2):
            unit_copy(n, which).wait_send()
    unit_across().wait_send()
    wait_sends(0, early_chunks)
    rows_copy.wait()
    every_copy.wait()
    unit_every.wait()
    unit_across().wait_recv()
    for c in range(early_chunks):
        unless(other_short, c, lambda c=c: stream_across(c).wait_recv())

    for c in range(chunks - LAG, chunks):
        take(c)

    for c in range(early_chunks, chunks):
        unless(other_short, c, lambda c=c: stream_across(c).wait_recv())

    pairs = slots // 2

    @pl.loop(0, rows_here * pairs, unroll=20)
    def _(step):
        t, pair = step // pairs, lax.rem(step, pairs)
        start = t * slots * slots + 2 * pair
        left = jnp.concatenate([rows_own[t * slots + k] for k in range(slots)], axis=1)
        rhs = jnp.concatenate([
            jnp.concatenate([every[place[start + k * slots]], every[place[start + k * slots + 1]]], axis=1)
            for k in range(slots)], axis=0)
        product = jnp.dot(left, rhs, preferred_element_type=jnp.float32).astype(out_ref.dtype)
        out_ref[t, 2 * pair] = product[:, :width]
        out_ref[t, 2 * pair + 1] = product[:, width:]

    wait_sends(early_chunks, chunks)


def sparse_square(sizes, table, values):
    rows_here, slots, half, width = values.shape
    blocks = rows_here * slots
    first_rows = rows_here // 2
    units = 2 * HOPS + 1
    chunks = (STREAM - first_rows * slots) // CHUNK
    crossings = rows_here + 1 + chunks

    def whole_blocks(count):
        return pltpu.VMEM((count, 2 * half, width), values.dtype)

    return pl.pallas_call(
        functools.partial(sparse_kernel, sizes),
        out_shape=[jax.ShapeDtypeStruct(values.shape, values.dtype), jax.ShapeDtypeStruct((1, 1), jnp.int32)],
        in_specs=[pl.BlockSpec(memory_space=pl.ANY), pl.BlockSpec(memory_space=pl.ANY)],
        out_specs=[pl.BlockSpec(memory_space=pltpu.VMEM), pl.BlockSpec(memory_space=pltpu.SMEM)],
        scratch_shapes=[
            pltpu.VMEM((blocks, half, width), values.dtype),
            whole_blocks(blocks),
            whole_blocks(blocks + STREAM),
            whole_blocks(blocks + 2 * STREAM + 1),
            whole_blocks(chunks * CHUNK),
            whole_blocks(chunks * CHUNK),
            pltpu.SMEM(table.shape, jnp.int32),
            pltpu.VMEM(table.shape, jnp.int32),
            pltpu.SMEM((units * rows_here,), jnp.int32),
            pltpu.SMEM(((HOPS + 1) * rows_here * 3,), jnp.int32),
            pltpu.SMEM((STREAM,), jnp.int32),
            pltpu.SMEM((units * blocks,), jnp.int32),
            pltpu.SMEM((blocks * slots,), jnp.int32),
            pltpu.SemaphoreType.DMA((first_rows, 2)),
            pltpu.SemaphoreType.DMA((first_rows, 2)),
            pltpu.SemaphoreType.DMA((chunks,)),
            pltpu.SemaphoreType.DMA((chunks,)),
            pltpu.SemaphoreType.DMA((crossings,)),
            pltpu.SemaphoreType.DMA((crossings,)),
            pltpu.SemaphoreType.DMA((7,)),
        ],
        compiler_params=pltpu.CompilerParams(
            collective_id=0, has_side_effects=True, vmem_limit_bytes=56 << 20),
        name="sparse_square",
    )(table, values.reshape(blocks, half, width))


def on_device(sizes, values, columns):
    table = columns.T
    square, excess = sparse_square(sizes, table, values)
    return lax.cond(excess[0, 0] > 0,
                    lambda: whole_square(sizes, table, values),
                    lambda: square)


def solution(mesh):
    return jax.shard_map(
        functools.partial(on_device, (mesh.shape["row"], mesh.shape["col"])),
        mesh=mesh,
        in_specs=(P(("row", "col"), None, "layer", None), P()),
        out_specs=P(("row", "col"), None, "layer", None),
        check_vma=False,
    )
```
